32 devices in a mesh: blk: 8 (over z, x), col: 4 (over y, core).
Axes of the slice: x: 2, y: 2, z: 4, core: 2. Of those that a mesh axis runs over, the one named last changes fastest.
Arguments:
- points: float32 [16, 8192], P(None, 'blk'), may hold values from -5 to 5
- lengths: float32 [16], replicated, may hold values from 2 to 4
- noise: float32 [8192], P('blk'), may hold values from 0.5 to 2
- outscale: float32 [1], replicated, may hold values from 0.02 to 0.1
- solution: float32 [32, 8192], P('col', 'blk'), may hold values from -6 to 6
- residual: float32 [32, 8192], P('col', 'blk'), may hold values from -26 to 26
- direction: float32 [32, 8192], P('col', 'blk'), may hold values from -31 to 31
Outputs:
- solution_next: float32 [32, 8192], P('col', 'blk')
- residual_next: float32 [32, 8192], P('col', 'blk')
- direction_next: float32 [32, 8192], P('col', 'blk')
The draws below stay inside these ranges and needn't reach their ends.
All inputs are finite; a program needn't handle non-finite values.
Results may differ from the reference program's by a relative error of at most 0.0003.
Values may be sent and summed in bfloat16 or wider, within the bound.
A program may use at most 64 MiB of HBM per device.

```python
import math
import jax
import jax.numpy as jnp
from jax import lax

DIM = 16
COLS = 32
POINTS = 8192


def field_scale():
    rows = jnp.arange(COLS, dtype=jnp.float32)[:, None]
    spots = jnp.arange(POINTS, dtype=jnp.float32)[None, :]
    return 0.2 * 10.0 ** (spots / (POINTS - 1)) * 10.0 ** (0.5 * rows / (COLS - 1))


def draw_residual(key, part):
    key = jax.random.fold_in(key, 11)
    values = jax.random.truncated_normal(key, -4.0, 4.0, (COLS, POINTS), jnp.float32)
    return values * field_scale()


def draw_direction(key, part):
    key = jax.random.fold_in(key, 23)
    signs = jax.random.randint(jax.random.fold_in(key, 7), (COLS, 1), 0, 2).astype(jnp.float32) * 2.0 - 1.0
    values = jax.random.truncated_normal(key, -4.0, 4.0, (COLS, POINTS), jnp.float32)
    values = values + 0.8 * signs
    return values * field_scale()


def steps_of(own_key, extent, split, low, top_value):
    gain, own = 1.0, jax.random.fold_in(own_key, 6)
    for dim, blocks in split:
        heights = jnp.exp(jax.random.uniform(jax.random.fold_in(own, dim), (blocks,), jnp.float32, low / len(split), top_value / len(split)))
        gain = gain * jnp.repeat(heights, extent[dim] // blocks).reshape([-1 if axis == dim else 1 for axis in range(len(extent))])
    return gain


def gaussian(rng, shape, spread, limit, shards=(), kind=jnp.bfloat16):
    values = jax.random.normal(rng, shape, jnp.float32) * spread
    if len(shards) > 0:
        values = steps_of(rng, shape, shards, -0.22, 0.18) * values
    return jnp.clip(values, min=-limit, max=limit).astype(kind)


def setup_inputs(seed: int = 0) -> dict:
    splits = jax.random.split(jax.random.key(seed), 8)
    points = gaussian(splits[0], (DIM, POINTS), 1.0, 5.0, ((1, 8),), jnp.float32)
    lengths = jnp.clip(jnp.exp(jax.random.uniform(splits[1], (DIM,), jnp.float32, math.log(2.0), math.log(4.0))), 2.0, 4.0)
    noise = jnp.clip(jnp.exp(math.log(2.0) - 1.3862944 * jax.random.uniform(splits[2], (POINTS,), jnp.float32) ** steps_of(splits[2], (POINTS,), ((0, 8),), -0.2, 0.2)), 0.5, 2.0)
    outscale = jnp.clip(jnp.exp(jax.random.uniform(splits[3], (1,), jnp.float32, math.log(0.02), math.log(0.1))), 0.02, 0.1)
    solution = gaussian(splits[4], (COLS, POINTS), 1.0, 6.0, ((0, 4), (1, 8)), jnp.float32)
    residual = draw_residual(jax.random.fold_in(splits[7], 71), 0)
    direction = draw_direction(jax.random.fold_in(splits[7], 71), 0)
    return {"points": points, "lengths": lengths, "noise": noise, "outscale": outscale, "solution": solution, "residual": residual, "direction": direction}


def matern_tile(left, right, amplitude):
    cross = lax.dot_general(left, right, (((0,), (0,)), ((), ())), precision=lax.Precision.HIGHEST, preferred_element_type=jnp.float32)
    left_sq = lax.optimization_barrier(jnp.sum(left * left, axis=0))
    right_sq = lax.optimization_barrier(jnp.sum(right * right, axis=0))
    dist_sq = jnp.maximum(left_sq[:, None] + right_sq[None, :] - 2.0 * cross, 0.0)
    radius = jnp.sqrt(5.0 * dist_sq)
    return (amplitude * (1.0 + radius + radius * radius / 3.0) * jnp.exp(-radius)).astype(jnp.bfloat16)

def reference(points, lengths, noise, outscale, solution, residual, direction):
    scaled = points / lengths[:, None]
    lowered = direction.astype(jnp.bfloat16)
    block_rows = math.gcd(POINTS, 512)
    count = POINTS // block_rows
    pieces = scaled.reshape(DIM, count, block_rows).transpose(1, 0, 2)

    def one_block(piece):
        kernel_tile = matern_tile(scaled, piece, outscale[0])
        return jnp.dot(lowered, kernel_tile, preferred_element_type=jnp.float32)
    products = lax.map(one_block, pieces)
    image = products.transpose(1, 0, 2).reshape(COLS, POINTS) + noise[None, :] * direction
    norm_now = lax.optimization_barrier(jnp.sum(residual * residual, axis=1))
    curve = lax.optimization_barrier(jnp.sum(direction * image, axis=1))
    alpha = norm_now / curve
    solution_next = solution + alpha[:, None] * direction
    residual_next = residual - alpha[:, None] * image
    norm_next = lax.optimization_barrier(jnp.sum(residual_next * residual_next, axis=1))
    direction_next = residual_next + (norm_next / norm_now)[:, None] * direction
    return (solution_next, residual_next, direction_next)
```

```python
import functools
import math

import jax
import jax.numpy as jnp
from jax import lax
from jax.experimental import pallas as pl
from jax.experimental.pallas import tpu as pltpu
from jax.sharding import PartitionSpec as P

MESH = pl.DeviceIdType.MESH
LOG2E = math.log2(math.e)
LN2 = math.log(2.0)
KAPPA = 5.0 * LOG2E * LOG2E
DEPTH = 64


def split3(x):
    first = x.astype(jnp.bfloat16).astype(jnp.float32)
    second = (x - first).astype(jnp.bfloat16).astype(jnp.float32)
    third = x - first - second
    return first, second, third


def extra_rows(rows, count):
    row = lax.broadcasted_iota(jnp.int32, (16, count), 0)
    block = jnp.zeros((16, count), jnp.float32)
    for index, value in enumerate(rows):
        block = jnp.where(row == index, value, block)
    return block.astype(jnp.bfloat16)


def kernel(
    nb, nc, tile,
    points, lengths, noise, outscale, solution, residual, direction,
    solution_next, residual_next, direction_next,
    low_own, pts_own, low_buf, pts_buf, far, near, kmat, part, part_in, stat, stat_in,
    low_send, low_recv, pts_send, pts_recv, part_send, part_recv, stat_send, stat_recv,
):
    b = lax.axis_index("blk")
    c = lax.axis_index("col")
    per = nb // nc
    dim, count = points.shape
    cols = direction.shape[0]
    half = count // 2
    tiles = count // tile
    quarter = b // per
    slot = b % per
    mine = quarter == c

    barrier = pltpu.get_barrier_semaphore()

    def greet(block, col):
        pl.semaphore_signal(barrier, inc=1, device_id=(block, col), device_id_type=MESH)

    def greet_sources(k, carry):
        block = c * per + k // nc
        col = k % nc

        @pl.when(jnp.logical_or(block != b, col != c))
        def _():
            greet(block, col)

        return carry

    lax.fori_loop(0, per * nc, greet_sources, 0)

    def greet_blocks(k, carry):
        greet((b + k) % nb, c)
        return carry

    lax.fori_loop(1, nb, greet_blocks, 0)
    for k in range(1, nc):
        greet(b, (c + k) % nc)

    row = lax.broadcasted_iota(jnp.int32, (dim, 128), 0)
    scale = jnp.zeros((dim, 128), jnp.float32)
    for k in range(dim):
        scale = jnp.where(row == k, lengths[k], scale)
    scaled = points[...] / scale[:, :1]
    pts_own[...] = scaled.astype(jnp.bfloat16)
    own = direction[...]
    low_own[...] = jnp.concatenate([own[:, :half], own[:, half:]], axis=0).astype(jnp.bfloat16)

    pl.semaphore_wait(
        barrier, nb - jnp.where(mine, 1, 0) + nb - 1 + nc - 1
    )

    def pts_copy(k):
        return pltpu.make_async_remote_copy(
            src_ref=pts_own, dst_ref=pts_buf.at[slot],
            send_sem=pts_send.at[k], recv_sem=pts_recv.at[slot],
            device_id=(k, quarter), device_id_type=MESH,
        )

    def low_copy(k):
        return pltpu.make_async_remote_copy(
            src_ref=low_own, dst_ref=low_buf.at[slot, c],
            send_sem=low_send.at[k], recv_sem=low_recv.at[slot, c],
            device_id=(k, quarter), device_id_type=MESH,
        )

    def each_pts(act):
        def step(k, carry):
            block = c + k * nc

            @pl.when(block != b)
            def _():
                act(pts_copy(block))

            return carry

        lax.fori_loop(0, per, step, 0)

    def each_low(act):
        def step(k, carry):
            block = (b + k) % nb

            @pl.when(jnp.logical_or(k != 0, jnp.logical_not(mine)))
            def _():
                act(low_copy(block))

            return carry

        lax.fori_loop(0, nb, step, 0)

    each_pts(lambda copy: copy.start())
    each_low(lambda copy: copy.start())

    @pl.when(mine)
    def _():
        pts_buf[slot] = pts_own[...]
        low_buf[slot, c] = low_own[...]

    first, second, third = split3(scaled * (-2.0 * KAPPA))
    norms = split3(KAPPA * jnp.sum(scaled * scaled, axis=0, keepdims=True))
    near[0:16, :] = first.astype(jnp.bfloat16)
    near[16:32, :] = second.astype(jnp.bfloat16)
    near[32:48, :] = third.astype(jnp.bfloat16)
    near[48:64, :] = extra_rows((1.0, 1.0, 1.0) + norms, count)

    amplitude = outscale[0]
    slope = amplitude * LN2
    bend = amplitude * (LN2 * LN2 / 3.0)

    def kernel_block(jb, carry):
        @pl.when(c * per + jb != b)
        def _():
            pltpu.make_async_copy(pts_buf.at[jb], pts_buf.at[jb], pts_recv.at[jb]).wait()

        other = pts_buf[jb]
        wide = other.astype(jnp.float32)
        squares = split3(KAPPA * jnp.sum(wide * wide, axis=0, keepdims=True))
        stacked = jnp.concatenate(
            [other, other, other, extra_rows(squares + (1.0, 1.0, 1.0), count)], axis=0
        )
        far[...] = stacked.T

        def kernel_tile(it, inner):
            cut = pl.ds(pl.multiple_of(it * tile, tile), tile)
            gap = jnp.dot(far[...], near[:, cut], preferred_element_type=jnp.float32)
            gap = jnp.maximum(gap, 1e-30)
            radius = gap * lax.rsqrt(gap)
            value = (amplitude + radius * (slope + radius * bend)) * jnp.exp2(-radius)
            kmat[jb, :, cut] = value.astype(jnp.bfloat16)
            return inner

        return lax.fori_loop(0, tiles, kernel_tile, carry)

    lax.fori_loop(0, per, kernel_block, 0)

    def wait_low(k, carry):
        jb = k // nc
        col = k % nc

        @pl.when(jnp.logical_or(c * per + jb != b, col != c))
        def _():
            pltpu.make_async_copy(
                low_buf.at[jb, col], low_buf.at[jb, col], low_recv.at[jb, col]
            ).wait()

        return carry

    lax.fori_loop(0, per * nc, wait_low, 0)

    def part_copy(it, col):
        cut = pl.ds(pl.multiple_of(it * tile, tile), tile)
        return pltpu.make_async_remote_copy(
            src_ref=part.at[col, :, cut], dst_ref=part_in.at[c, :, cut],
            send_sem=part_send.at[it, col], recv_sem=part_recv.at[it, c],
            device_id=(b, col), device_id_type=MESH,
        )

    def image_tile(it, carry):
        cut = pl.ds(pl.multiple_of(it * tile, tile), tile)

        def image_block(jb, total):
            shards = []
            for col in range(nc):
                wide = low_buf[jb, col].astype(jnp.float32)
                shards.append(jnp.concatenate([wide[:cols], wide[cols:]], axis=1))
            low = jnp.concatenate(shards, axis=0).astype(jnp.bfloat16)
            return total + jnp.dot(low, kmat[jb, :, cut], preferred_element_type=jnp.float32)

        total = lax.fori_loop(0, per, image_block, jnp.zeros((nc * cols, tile), jnp.float32))
        for col in range(nc):
            part[col, :, cut] = total[col * cols : (col + 1) * cols]
        for k in range(1, nc):
            part_copy(it, (c + k) % nc).start()
        return carry

    lax.fori_loop(0, tiles, image_tile, 0)

    now = residual[...]
    image = part[c] + noise[...] * own
    for k in range(1, nc):
        col = (c + k) % nc
        for it in range(tiles):
            cut = pl.ds(it * tile, tile)
            pltpu.make_async_copy(
                part_in.at[col, :, cut], part_in.at[col, :, cut], part_recv.at[it, col]
            ).wait()
        image = image + part_in[col]

    lane = lax.broadcasted_iota(jnp.int32, (cols, 128), 1)
    sums = jnp.zeros((cols, 128), jnp.float32)
    for index, product in enumerate((own * image, now * image, image * image, now * now)):
        sums = jnp.where(lane == index, jnp.sum(product, axis=1, keepdims=True), sums)
    stat[...] = sums

    def stat_copy(block):
        return pltpu.make_async_remote_copy(
            src_ref=stat, dst_ref=stat_in.at[b],
            send_sem=stat_send.at[block], recv_sem=stat_recv.at[b],
            device_id=(block, c), device_id_type=MESH,
        )

    def start_stat(k, carry):
        stat_copy((b + k) % nb).start()
        return carry

    lax.fori_loop(1, nb, start_stat, 0)

    def add_stat(k, total):
        block = (b + k) % nb
        pltpu.make_async_copy(stat_in.at[block], stat_in.at[block], stat_recv.at[block]).wait()
        return total + stat_in[block]

    sums = lax.fori_loop(1, nb, add_stat, sums)
    curve, mixed, power, norm_now = (sums[:, index : index + 1] for index in range(4))
    alpha = norm_now / curve
    norm_next = norm_now - 2.0 * alpha * mixed + alpha * alpha * power
    after = now - alpha * image
    solution_next[...] = solution[...] + alpha * own
    residual_next[...] = after
    direction_next[...] = after + (norm_next / norm_now) * own

    each_pts(lambda copy: copy.wait_send())
    each_low(lambda copy: copy.wait_send())

    def sent_part(k, carry):
        part_copy(k // (nc - 1), (c + 1 + k % (nc - 1)) % nc).wait_send()
        return carry

    lax.fori_loop(0, tiles * (nc - 1), sent_part, 0)

    def sent_stat(k, carry):
        stat_copy((b + k) % nb).wait_send()
        return carry

    lax.fori_loop(1, nb, sent_stat, 0)


def local(nb, nc, points, lengths, noise, outscale, solution, residual, direction):
    dim, count = points.shape
    cols = direction.shape[0]
    per = nb // nc
    tile = math.gcd(count, 256)
    tiles = count // tile
    vmem = pl.BlockSpec(memory_space=pltpu.VMEM)
    smem = pl.BlockSpec(memory_space=pltpu.SMEM)
    state = jax.ShapeDtypeStruct((cols, count), jnp.float32)
    dma = pltpu.SemaphoreType.DMA
    entries = per * count * count
    return pl.pallas_call(
        functools.partial(kernel, nb, nc, tile),
        out_shape=(state, state, state),
        in_specs=[vmem, smem, vmem, smem, vmem, vmem, vmem],
        out_specs=(vmem, vmem, vmem),
        scratch_shapes=[
            pltpu.VMEM((2 * cols, count // 2), jnp.bfloat16),
            pltpu.VMEM((dim, count), jnp.bfloat16),
            pltpu.VMEM((per, nc, 2 * cols, count // 2), jnp.bfloat16),
            pltpu.VMEM((per, dim, count), jnp.bfloat16),
            pltpu.VMEM((count, DEPTH), jnp.bfloat16),
            pltpu.VMEM((DEPTH, count), jnp.bfloat16),
            pltpu.VMEM((per, count, count), jnp.bfloat16),
            pltpu.VMEM((nc, cols, count), jnp.float32),
            pltpu.VMEM((nc, cols, count), jnp.float32),
            pltpu.VMEM((cols, 128), jnp.float32),
            pltpu.VMEM((nb, cols, 128), jnp.float32),
            dma((nb,)), dma((per, nc)), dma((nb,)), dma((per,)),
            dma((tiles, nc)), dma((tiles, nc)), dma((nb,)), dma((nb,)),
        ],
        compiler_params=pltpu.CompilerParams(
            collective_id=0, has_side_effects=True, vmem_limit_bytes=56 * 1024 * 1024
        ),
        cost_estimate=pl.CostEstimate(
            flops=2 * entries * (DEPTH + nc * cols), bytes_accessed=1 << 19, transcendentals=2 * entries
        ),
    )(points, lengths, noise.reshape(1, count), outscale, solution, residual, direction)


def solution(mesh):
    in_specs = (
        P(None, "blk"), P(), P("blk"), P(),
        P("col", "blk"), P("col", "blk"), P("col", "blk"),
    )
    out_specs = (P("col", "blk"), P("col", "blk"), P("col", "blk"))
    body = functools.partial(local, mesh.shape["blk"], mesh.shape["col"])
    return jax.shard_map(body, mesh=mesh, in_specs=in_specs, out_specs=out_specs, check_vma=False)
```

```python
import functools
import math

import jax
import jax.numpy as jnp
from jax import lax
from jax.experimental import pallas as pl
from jax.experimental.pallas import tpu as pltpu
from jax.sharding import PartitionSpec as P

MESH = pl.DeviceIdType.MESH
LOG2E = math.log2(math.e)
LN2 = math.log(2.0)
KAPPA = 5.0 * LOG2E * LOG2E
DEPTH = 64


def split3(x):
    first = x.astype(jnp.bfloat16).astype(jnp.float32)
    second = (x - first).astype(jnp.bfloat16).astype(jnp.float32)
    third = x - first - second
    return first, second, third


def extra_rows(rows, count):
    row = lax.broadcasted_iota(jnp.int32, (16, count), 0)
    block = jnp.zeros((16, count), jnp.float32)
    for index, value in enumerate(rows):
        block = jnp.where(row == index, value, block)
    return block.astype(jnp.bfloat16)


def kernel(
    nb, nc, tile,
    points_in, lengths_in, noise_in, outscale_in, residual_in, direction_in,
    image_out, sums_out,
    points, lengths, noise, outscale, residual, direction, in_sems,
    low_own, pts_own, low_buf, pts_buf, far, near, kmat, part, part_in, stat, stat_in,
    low_send, low_recv, pts_send, pts_recv, part_send, part_recv, stat_send, stat_recv,
):
    b = lax.axis_index("blk")
    c = lax.axis_index("col")
    per = nb // nc
    dim, count = points.shape
    cols = direction.shape[0]
    half = count // 2
    tiles = count // tile
    quarter = b // per
    slot = b % per
    mine = quarter == c

    loads = [
        pltpu.make_async_copy(source, target, in_sems.at[index])
        for index, (source, target) in enumerate(
            (
                (points_in, points), (lengths_in, lengths), (direction_in, direction),
                (noise_in, noise), (outscale_in, outscale), (residual_in, residual),
            )
        )
    ]
    for load in loads:
        load.start()

    barrier = pltpu.get_barrier_semaphore()

    def greet(block, col):
        pl.semaphore_signal(barrier, inc=1, device_id=(block, col), device_id_type=MESH)

    def greet_sources(k, carry):
        block = c * per + k // nc
        col = k % nc

        @pl.when(jnp.logical_or(block != b, col != c))
        def _():
            greet(block, col)

        return carry

    lax.fori_loop(0, per * nc, greet_sources, 0)

    def greet_blocks(k, carry):
        greet((b + k) % nb, c)
        return carry

    lax.fori_loop(1, nb, greet_blocks, 0)
    for k in range(1, nc):
        greet(b, (c + k) % nc)

    for load in loads:
        load.wait()
    row = lax.broadcasted_iota(jnp.int32, (dim, 128), 0)
    scale = jnp.zeros((dim, 128), jnp.float32)
    for k in range(dim):
        scale = jnp.where(row == k, lengths[k], scale)
    scaled = points[...] / scale[:, :1]
    pts_own[...] = scaled.astype(jnp.bfloat16)
    own = direction[...]
    low_own[...] = jnp.concatenate([own[:, :half], own[:, half:]], axis=0).astype(jnp.bfloat16)

    pl.semaphore_wait(
        barrier, nb - jnp.where(mine, 1, 0) + nb - 1 + nc - 1
    )

    def pts_copy(k):
        return pltpu.make_async_remote_copy(
            src_ref=pts_own, dst_ref=pts_buf.at[slot],
            send_sem=pts_send.at[k], recv_sem=pts_recv.at[slot],
            device_id=(k, quarter), device_id_type=MESH,
        )

    def low_copy(k):
        return pltpu.make_async_remote_copy(
            src_ref=low_own, dst_ref=low_buf.at[slot, c],
            send_sem=low_send.at[k], recv_sem=low_recv.at[slot, c],
            device_id=(k, quarter), device_id_type=MESH,
        )

    def each_pts(act):
        def step(k, carry):
            block = c + k * nc

            @pl.when(block != b)
            def _():
                act(pts_copy(block))

            return carry

        lax.fori_loop(0, per, step, 0)

    def each_low(act):
        def step(k, carry):
            block = (b + k) % nb

            @pl.when(jnp.logical_or(k != 0, jnp.logical_not(mine)))
            def _():
                act(low_copy(block))

            return carry

        lax.fori_loop(0, nb, step, 0)

    each_pts(lambda copy: copy.start())
    each_low(lambda copy: copy.start())

    @pl.when(mine)
    def _():
        pts_buf[slot] = pts_own[...]
        low_buf[slot, c] = low_own[...]

    first, second, third = split3(scaled * (-2.0 * KAPPA))
    norms = split3(KAPPA * jnp.sum(scaled * scaled, axis=0, keepdims=True))
    near[0:16, :] = first.astype(jnp.bfloat16)
    near[16:32, :] = second.astype(jnp.bfloat16)
    near[32:48, :] = third.astype(jnp.bfloat16)
    near[48:64, :] = extra_rows((1.0, 1.0, 1.0) + norms, count)

    amplitude = outscale[...]
    slope = amplitude * LN2
    bend = amplitude * (LN2 * LN2 / 3.0)

    def kernel_block(jb, carry):
        @pl.when(c * per + jb != b)
        def _():
            pltpu.make_async_copy(pts_buf.at[jb], pts_buf.at[jb], pts_recv.at[jb]).wait()

        other = pts_buf[jb]
        wide = other.astype(jnp.float32)
        squares = split3(KAPPA * jnp.sum(wide * wide, axis=0, keepdims=True))
        stacked = jnp.concatenate(
            [other, other, other, extra_rows(squares + (1.0, 1.0, 1.0), count)], axis=0
        )
        far[...] = stacked.T

        def kernel_tile(it, inner):
            cut = pl.ds(pl.multiple_of(it * tile, tile), tile)
            gap = jnp.dot(far[...], near[:, cut], preferred_element_type=jnp.float32)
            gap = jnp.maximum(gap, 1e-30)
            radius = gap * lax.rsqrt(gap)
            value = (amplitude + radius * (slope + radius * bend)) * jnp.exp2(-radius)
            kmat[jb, :, cut] = value.astype(jnp.bfloat16)
            return inner

        return lax.fori_loop(0, tiles, kernel_tile, carry)

    lax.fori_loop(0, per, kernel_block, 0)

    def wait_low(k, carry):
        jb = k // nc
        col = k % nc

        @pl.when(jnp.logical_or(c * per + jb != b, col != c))
        def _():
            pltpu.make_async_copy(
                low_buf.at[jb, col], low_buf.at[jb, col], low_recv.at[jb, col]
            ).wait()

        return carry

    lax.fori_loop(0, per * nc, wait_low, 0)

    def part_copy(it, col):
        cut = pl.ds(pl.multiple_of(it * tile, tile), tile)
        return pltpu.make_async_remote_copy(
            src_ref=part.at[col, :, cut], dst_ref=part_in.at[c, :, cut],
            send_sem=part_send.at[it, col], recv_sem=part_recv.at[it, c],
            device_id=(b, col), device_id_type=MESH,
        )

    def image_tile(it, carry):
        cut = pl.ds(pl.multiple_of(it * tile, tile), tile)

        def image_block(jb, total):
            shards = []
            for col in range(nc):
                wide = low_buf[jb, col].astype(jnp.float32)
                shards.append(jnp.concatenate([wide[:cols], wide[cols:]], axis=1))
            low = jnp.concatenate(shards, axis=0).astype(jnp.bfloat16)
            return total + jnp.dot(low, kmat[jb, :, cut], preferred_element_type=jnp.float32)

        total = lax.fori_loop(0, per, image_block, jnp.zeros((nc * cols, tile), jnp.float32))
        for col in range(nc):
            part[col, :, cut] = total[col * cols : (col + 1) * cols]
        for k in range(1, nc):
            part_copy(it, (c + k) % nc).start()
        return carry

    lax.fori_loop(0, tiles, image_tile, 0)

    now = residual[...]
    image = part[c] + noise[...] * own
    for k in range(1, nc):
        col = (c + k) % nc
        for it in range(tiles):
            cut = pl.ds(it * tile, tile)
            pltpu.make_async_copy(
                part_in.at[col, :, cut], part_in.at[col, :, cut], part_recv.at[it, col]
            ).wait()
        image = image + part_in[col]

    lane = lax.broadcasted_iota(jnp.int32, (cols, 128), 1)
    sums = jnp.zeros((cols, 128), jnp.float32)
    for index, product in enumerate((own * image, now * image, image * image, now * now)):
        sums = jnp.where(lane == index, jnp.sum(product, axis=1, keepdims=True), sums)
    stat[...] = sums

    def stat_copy(block):
        return pltpu.make_async_remote_copy(
            src_ref=stat, dst_ref=stat_in.at[b],
            send_sem=stat_send.at[block], recv_sem=stat_recv.at[b],
            device_id=(block, c), device_id_type=MESH,
        )

    def start_stat(k, carry):
        stat_copy((b + k) % nb).start()
        return carry

    lax.fori_loop(1, nb, start_stat, 0)

    def add_stat(k, total):
        block = (b + k) % nb
        pltpu.make_async_copy(stat_in.at[block], stat_in.at[block], stat_recv.at[block]).wait()
        return total + stat_in[block]

    sums = lax.fori_loop(1, nb, add_stat, sums)
    image_out[...] = image
    sums_out[...] = sums

    each_pts(lambda copy: copy.wait_send())
    each_low(lambda copy: copy.wait_send())

    def sent_part(k, carry):
        part_copy(k // (nc - 1), (c + 1 + k % (nc - 1)) % nc).wait_send()
        return carry

    lax.fori_loop(0, tiles * (nc - 1), sent_part, 0)

    def sent_stat(k, carry):
        stat_copy((b + k) % nb).wait_send()
        return carry

    lax.fori_loop(1, nb, sent_stat, 0)


def local(nb, nc, points, lengths, noise, outscale, solution, residual, direction):
    dim, count = points.shape
    cols = direction.shape[0]
    per = nb // nc
    tile = math.gcd(count, 256)
    tiles = count // tile
    vmem = pl.BlockSpec(memory_space=pltpu.VMEM)
    state = jax.ShapeDtypeStruct((cols, count), jnp.float32)
    totals = jax.ShapeDtypeStruct((cols, 128), jnp.float32)
    here = pl.BlockSpec(memory_space=pl.ANY)
    dma = pltpu.SemaphoreType.DMA
    entries = per * count * count
    image, sums = pl.pallas_call(
        functools.partial(kernel, nb, nc, tile),
        out_shape=(state, totals),
        in_specs=[here] * 6,
        out_specs=(vmem, vmem),
        scratch_shapes=[
            pltpu.VMEM((dim, count), jnp.float32),
            pltpu.SMEM((dim,), jnp.float32),
            pltpu.VMEM((1, count), jnp.float32),
            pltpu.VMEM((1, 1), jnp.float32),
            pltpu.VMEM((cols, count), jnp.float32),
            pltpu.VMEM((cols, count), jnp.float32),
            dma((6,)),
            pltpu.VMEM((2 * cols, count // 2), jnp.bfloat16),
            pltpu.VMEM((dim, count), jnp.bfloat16),
            pltpu.VMEM((per, nc, 2 * cols, count // 2), jnp.bfloat16),
            pltpu.VMEM((per, dim, count), jnp.bfloat16),
            pltpu.VMEM((count, DEPTH), jnp.bfloat16),
            pltpu.VMEM((DEPTH, count), jnp.bfloat16),
            pltpu.VMEM((per, count, count), jnp.bfloat16),
            pltpu.VMEM((nc, cols, count), jnp.float32),
            pltpu.VMEM((nc, cols, count), jnp.float32),
            pltpu.VMEM((cols, 128), jnp.float32),
            pltpu.VMEM((nb, cols, 128), jnp.float32),
            dma((nb,)), dma((per, nc)), dma((nb,)), dma((per,)),
            dma((tiles, nc)), dma((tiles, nc)), dma((nb,)), dma((nb,)),
        ],
        compiler_params=pltpu.CompilerParams(
            collective_id=0, has_side_effects=True, vmem_limit_bytes=56 * 1024 * 1024
        ),
        cost_estimate=pl.CostEstimate(
            flops=2 * entries * (DEPTH + nc * cols), bytes_accessed=1 << 19, transcendentals=2 * entries
        ),
    )(points, lengths, noise.reshape(1, count), outscale.reshape(1, 1), residual, direction)
    curve, mixed, power, norm_now = (sums[:, index : index + 1] for index in range(4))
    alpha = norm_now / curve
    norm_next = norm_now - 2.0 * alpha * mixed + alpha * alpha * power
    after = residual - alpha * image
    return (
        solution + alpha * direction,
        after,
        after + (norm_next / norm_now) * direction,
    )


def solution(mesh):
    in_specs = (
        P(None, "blk"), P(), P("blk"), P(),
        P("col", "blk"), P("col", "blk"), P("col", "blk"),
    )
    out_specs = (P("col", "blk"), P("col", "blk"), P("col", "blk"))
    body = functools.partial(local, mesh.shape["blk"], mesh.shape["col"])
    return jax.shard_map(body, mesh=mesh, in_specs=in_specs, out_specs=out_specs, check_vma=False)
```

```python
import functools
import math

import jax
import jax.numpy as jnp
from jax import lax
from jax.experimental import pallas as pl
from jax.experimental.pallas import tpu as pltpu
from jax.sharding import PartitionSpec as P

MESH = pl.DeviceIdType.MESH
LOG2E = math.log2(math.e)
LN2 = math.log(2.0)
KAPPA = 5.0 * LOG2E * LOG2E
DEPTH = 64


def split3(x):
    first = x.astype(jnp.bfloat16).astype(jnp.float32)
    second = (x - first).astype(jnp.bfloat16).astype(jnp.float32)
    third = x - first - second
    return first, second, third


def extra_rows(rows, count):
    row = lax.broadcasted_iota(jnp.int32, (16, count), 0)
    block = jnp.zeros((16, count), jnp.float32)
    for index, value in enumerate(rows):
        block = jnp.where(row == index, value, block)
    return block.astype(jnp.bfloat16)


def kernel(
    nb, nc, tile,
    points_in, lengths_in, noise_in, outscale_in, residual_in, direction_in,
    step_out, drop_out, keep_out,
    points, lengths, noise, outscale, residual, direction, in_sems,
    low_own, pts_own, low_buf, pts_buf, far, near, low_all, kmat_a, kmat_b, part, part_in, stat, stat_in,
    low_send, low_recv, pts_send, pts_recv, part_send, part_recv, stat_send, stat_recv,
):
    b = lax.axis_index("blk")
    c = lax.axis_index("col")
    per = nb // nc
    dim, count = points.shape
    cols = direction.shape[0]
    half = count // 2
    tiles = count // tile
    quarter = b // per
    slot = b % per
    mine = quarter == c

    loads = [
        pltpu.make_async_copy(source, target, in_sems.at[index])
        for index, (source, target) in enumerate(
            (
                (points_in, points), (lengths_in, lengths), (direction_in, direction),
                (noise_in, noise), (outscale_in, outscale), (residual_in, residual),
            )
        )
    ]
    for load in loads:
        load.start()

    barrier = pltpu.get_barrier_semaphore()

    def greet(block, col):
        pl.semaphore_signal(barrier, inc=1, device_id=(block, col), device_id_type=MESH)

    def greet_sources(k, carry):
        block = c * per + k // nc
        col = k % nc

        @pl.when(jnp.logical_or(block != b, col != c))
        def _():
            greet(block, col)

        return carry

    lax.fori_loop(0, per * nc, greet_sources, 0)

    def greet_blocks(k, carry):
        greet((b + k) % nb, c)
        return carry

    lax.fori_loop(1, nb, greet_blocks, 0)
    for k in range(1, nc):
        greet(b, (c + k) % nc)

    for load in loads:
        load.wait()
    row = lax.broadcasted_iota(jnp.int32, (dim, 128), 0)
    scale = jnp.zeros((dim, 128), jnp.float32)
    for k in range(dim):
        scale = jnp.where(row == k, lengths[k], scale)
    scaled = points[...] / scale[:, :1]
    pts_own[...] = scaled.astype(jnp.bfloat16)
    own = direction[...]
    low_own[...] = jnp.concatenate([own[:, :half], own[:, half:]], axis=0).astype(jnp.bfloat16)

    pl.semaphore_wait(
        barrier, nb - jnp.where(mine, 1, 0) + nb - 1 + nc - 1
    )

    def pts_copy(k):
        return pltpu.make_async_remote_copy(
            src_ref=pts_own, dst_ref=pts_buf.at[slot],
            send_sem=pts_send.at[k], recv_sem=pts_recv.at[slot],
            device_id=(k, quarter), device_id_type=MESH,
        )

    def low_copy(k):
        return pltpu.make_async_remote_copy(
            src_ref=low_own, dst_ref=low_buf.at[slot, c],
            send_sem=low_send.at[k], recv_sem=low_recv.at[slot, c],
            device_id=(k, quarter), device_id_type=MESH,
        )

    def each_pts(act):
        def step(k, carry):
            block = c + k * nc

            @pl.when(block != b)
            def _():
                act(pts_copy(block))

            return carry

        lax.fori_loop(0, per, step, 0)

    def each_low(act):
        def step(k, carry):
            block = (b + k) % nb

            @pl.when(jnp.logical_or(k != 0, jnp.logical_not(mine)))
            def _():
                act(low_copy(block))

            return carry

        lax.fori_loop(0, nb, step, 0)

    each_pts(lambda copy: copy.start())
    each_low(lambda copy: copy.start())

    @pl.when(mine)
    def _():
        pts_buf[slot] = pts_own[...]
        low_buf[slot, c] = low_own[...]

    first, second, third = split3(scaled * (-2.0 * KAPPA))
    norms = split3(KAPPA * jnp.sum(scaled * scaled, axis=0, keepdims=True))
    near[0:16, :] = first.astype(jnp.bfloat16)
    near[16:32, :] = second.astype(jnp.bfloat16)
    near[32:48, :] = third.astype(jnp.bfloat16)
    near[48:64, :] = extra_rows((1.0, 1.0, 1.0) + norms, count)

    shift = jnp.log(outscale[...] * (LN2 * LN2 / 3.0)) * LOG2E

    def form(jb):
        @pl.when(c * per + jb != b)
        def _():
            pltpu.make_async_copy(pts_buf.at[jb], pts_buf.at[jb], pts_recv.at[jb]).wait()

        other = pts_buf[jb]
        wide = other.astype(jnp.float32)
        squares = split3(KAPPA * jnp.sum(wide * wide, axis=0, keepdims=True))
        stacked = jnp.concatenate(
            [other, other, other, extra_rows(squares + (1.0, 1.0, 1.0), count)], axis=0
        )
        far[...] = stacked.T

    def fill(it, kmat):
        cut = slice(it * tile, (it + 1) * tile)
        gap = jnp.dot(far[...], near[:, cut], preferred_element_type=jnp.float32)
        gap = jnp.maximum(gap, 1e-30)
        radius = gap * lax.rsqrt(gap)
        value = ((radius + 3.0 / LN2) * radius + 3.0 / (LN2 * LN2)) * jnp.exp2(shift - radius)
        kmat[:, cut] = value.astype(jnp.bfloat16)

    def wait_low(jb):
        for col in range(nc):
            @pl.when(jnp.logical_or(c * per + jb != b, c != col))
            def _():
                pltpu.make_async_copy(
                    low_buf.at[jb, col], low_buf.at[jb, col], low_recv.at[jb, col]
                ).wait()

        shards = []
        for col in range(nc):
            wide = low_buf[jb, col].astype(jnp.float32)
            shards.append(jnp.concatenate([wide[:cols], wide[cols:]], axis=1))
        low_all[...] = jnp.concatenate(shards, axis=0).astype(jnp.bfloat16)

    def add_image(it, kmat, first):
        cut = slice(it * tile, (it + 1) * tile)
        total = jnp.dot(low_all[...], kmat[:, cut], preferred_element_type=jnp.float32)
        for col in range(nc):
            rows = total[col * cols : (col + 1) * cols]
            part[col, :, cut] = rows if first else part[col, :, cut] + rows

    def both(jb, now_mat, last_mat, first):
        form(jb)
        wait_low(jb - 1)
        for it in range(tiles):
            fill(it, now_mat)
            add_image(it, last_mat, first)

    form(0)
    for it in range(tiles):
        fill(it, kmat_a)
    both(1, kmat_b, kmat_a, True)

    def pair(p, carry):
        both(2 * p, kmat_a, kmat_b, False)
        both(2 * p + 1, kmat_b, kmat_a, False)
        return carry

    if per > 2:
        lax.fori_loop(1, per // 2, pair, 0)

    def part_copy(it, col):
        cut = pl.ds(pl.multiple_of(it * tile, tile), tile)
        return pltpu.make_async_remote_copy(
            src_ref=part.at[col, :, cut], dst_ref=part_in.at[c, :, cut],
            send_sem=part_send.at[it, col], recv_sem=part_recv.at[it, c],
            device_id=(b, col), device_id_type=MESH,
        )

    wait_low(per - 1)
    for it in range(tiles):
        add_image(it, kmat_b, False)
        for k in range(1, nc):
            part_copy(it, (c + k) % nc).start()

    now = residual[...]
    image = part[c] + noise[...] * own
    for k in range(1, nc):
        col = (c + k) % nc
        for it in range(tiles):
            cut = pl.ds(it * tile, tile)
            pltpu.make_async_copy(
                part_in.at[col, :, cut], part_in.at[col, :, cut], part_recv.at[it, col]
            ).wait()
        image = image + part_in[col]

    lane = lax.broadcasted_iota(jnp.int32, (cols, 128), 1)
    sums = jnp.zeros((cols, 128), jnp.float32)
    for index, product in enumerate((own * image, now * image, image * image, now * now)):
        sums = jnp.where(lane == index, jnp.sum(product, axis=1, keepdims=True), sums)
    stat[...] = sums

    def stat_copy(block):
        return pltpu.make_async_remote_copy(
            src_ref=stat, dst_ref=stat_in.at[b],
            send_sem=stat_send.at[block], recv_sem=stat_recv.at[b],
            device_id=(block, c), device_id_type=MESH,
        )

    def start_stat(k, carry):
        stat_copy((b + k) % nb).start()
        return carry

    lax.fori_loop(1, nb, start_stat, 0)

    def add_stat(k, total):
        block = (b + k) % nb
        pltpu.make_async_copy(stat_in.at[block], stat_in.at[block], stat_recv.at[block]).wait()
        return total + stat_in[block]

    sums = lax.fori_loop(1, nb, add_stat, sums)
    curve, mixed, power, norm_now = (sums[:, index : index + 1] for index in range(4))
    alpha = norm_now / curve
    norm_next = norm_now - 2.0 * alpha * mixed + alpha * alpha * power
    step_out[...] = alpha * own
    drop_out[...] = alpha * image
    keep_out[...] = (norm_next / norm_now) * own

    each_pts(lambda copy: copy.wait_send())
    each_low(lambda copy: copy.wait_send())

    def sent_part(k, carry):
        part_copy(k // (nc - 1), (c + 1 + k % (nc - 1)) % nc).wait_send()
        return carry

    lax.fori_loop(0, tiles * (nc - 1), sent_part, 0)

    def sent_stat(k, carry):
        stat_copy((b + k) % nb).wait_send()
        return carry

    lax.fori_loop(1, nb, sent_stat, 0)


def local(nb, nc, points, lengths, noise, outscale, solution, residual, direction):
    dim, count = points.shape
    cols = direction.shape[0]
    per = nb // nc
    tile = math.gcd(count, 256)
    tiles = count // tile
    vmem = pl.BlockSpec(memory_space=pltpu.VMEM)
    state = jax.ShapeDtypeStruct((cols, count), jnp.float32)
    here = pl.BlockSpec(memory_space=pl.ANY)
    dma = pltpu.SemaphoreType.DMA
    entries = per * count * count
    step, drop, keep = pl.pallas_call(
        functools.partial(kernel, nb, nc, tile),
        out_shape=(state, state, state),
        in_specs=[here] * 6,
        out_specs=(vmem, vmem, vmem),
        scratch_shapes=[
            pltpu.VMEM((dim, count), jnp.float32),
            pltpu.SMEM((dim,), jnp.float32),
            pltpu.VMEM((1, count), jnp.float32),
            pltpu.VMEM((1, 1), jnp.float32),
            pltpu.VMEM((cols, count), jnp.float32),
            pltpu.VMEM((cols, count), jnp.float32),
            dma((6,)),
            pltpu.VMEM((2 * cols, count // 2), jnp.bfloat16),
            pltpu.VMEM((dim, count), jnp.bfloat16),
            pltpu.VMEM((per, nc, 2 * cols, count // 2), jnp.bfloat16),
            pltpu.VMEM((per, dim, count), jnp.bfloat16),
            pltpu.VMEM((count, DEPTH), jnp.bfloat16),
            pltpu.VMEM((DEPTH, count), jnp.bfloat16),
            pltpu.VMEM((nc * cols, count), jnp.bfloat16),
            pltpu.VMEM((count, count), jnp.bfloat16),
            pltpu.VMEM((count, count), jnp.bfloat16),
            pltpu.VMEM((nc, cols, count), jnp.float32),
            pltpu.VMEM((nc, cols, count), jnp.float32),
            pltpu.VMEM((cols, 128), jnp.float32),
            pltpu.VMEM((nb, cols, 128), jnp.float32),
            dma((nb,)), dma((per, nc)), dma((nb,)), dma((per,)),
            dma((tiles, nc)), dma((tiles, nc)), dma((nb,)), dma((nb,)),
        ],
        compiler_params=pltpu.CompilerParams(
            collective_id=0, has_side_effects=True, vmem_limit_bytes=56 * 1024 * 1024
        ),
        cost_estimate=pl.CostEstimate(
            flops=2 * entries * (DEPTH + nc * cols), bytes_accessed=1 << 19, transcendentals=2 * entries
        ),
    )(points, lengths, noise.reshape(1, count), outscale.reshape(1, 1), residual, direction)
    after = residual - drop
    return (solution + step, after, after + keep)


def solution(mesh):
    in_specs = (
        P(None, "blk"), P(), P("blk"), P(),
        P("col", "blk"), P("col", "blk"), P("col", "blk"),
    )
    out_specs = (P("col", "blk"), P("col", "blk"), P("col", "blk"))
    body = functools.partial(local, mesh.shape["blk"], mesh.shape["col"])
    return jax.shard_map(body, mesh=mesh, in_specs=in_specs, out_specs=out_specs, check_vma=False)
```

```python
import functools
import math

import jax
import jax.numpy as jnp
from jax import lax
from jax.experimental import pallas as pl
from jax.experimental.pallas import tpu as pltpu
from jax.sharding import PartitionSpec as P

MESH = pl.DeviceIdType.MESH
LOG2E = math.log2(math.e)
LN2 = math.log(2.0)
KAPPA = 5.0 * LOG2E * LOG2E
DEPTH = 64


def spread(col, nc):
    return (col % 2) * (nc // 2) + col // 2


def gather_place(quarter, nc):
    return (quarter % (nc // 2)) * 2 + quarter // (nc // 2)


def split3(x):
    first = x.astype(jnp.bfloat16).astype(jnp.float32)
    second = (x - first).astype(jnp.bfloat16).astype(jnp.float32)
    third = x - first - second
    return first, second, third


def extra_rows(rows, count):
    row = lax.broadcasted_iota(jnp.int32, (16, count), 0)
    block = jnp.zeros((16, count), jnp.float32)
    for index, value in enumerate(rows):
        block = jnp.where(row == index, value, block)
    return block.astype(jnp.bfloat16)


def kernel(
    nb, nc, tile,
    points_in, lengths_in, noise_in, outscale_in, residual_in, direction_in,
    changes,
    points, lengths, noise, outscale, residual, direction, in_sems,
    low_own, pts_own, low_buf, pts_buf, far, near, low_all, kmat_a, kmat_b, part, part_in, stat, stat_in,
    low_send, low_recv, pts_send, pts_recv, part_send, part_recv, stat_send, stat_recv,
):
    b = lax.axis_index("blk")
    c = lax.axis_index("col")
    per = nb // nc
    dim, count = points.shape
    cols = direction.shape[0]
    half = count // 2
    tiles = count // tile
    keeper = gather_place(b // per, nc)
    base = spread(c, nc) * per
    slot = b % per
    mine = keeper == c

    loads = [
        pltpu.make_async_copy(source, target, in_sems.at[index])
        for index, (source, target) in enumerate(
            (
                (points_in, points), (lengths_in, lengths), (direction_in, direction),
                (noise_in, noise), (outscale_in, outscale), (residual_in, residual),
            )
        )
    ]
    for load in loads:
        load.start()

    barrier = pltpu.get_barrier_semaphore()

    def greet(block, col):
        pl.semaphore_signal(barrier, inc=1, device_id=(block, col), device_id_type=MESH)

    def greet_sources(k, carry):
        block = base + k // nc
        col = k % nc

        @pl.when(jnp.logical_or(block != b, col != c))
        def _():
            greet(block, col)

        return carry

    lax.fori_loop(0, per * nc, greet_sources, 0)

    def greet_blocks(k, carry):
        greet((b + k) % nb, c)
        return carry

    lax.fori_loop(1, nb, greet_blocks, 0)
    for k in range(1, nc):
        greet(b, (c + k) % nc)

    for load in loads:
        load.wait()
    row = lax.broadcasted_iota(jnp.int32, (dim, 128), 0)
    scale = jnp.zeros((dim, 128), jnp.float32)
    for k in range(dim):
        scale = jnp.where(row == k, lengths[k], scale)
    scaled = points[...] / scale[:, :1]
    pts_own[...] = scaled.astype(jnp.bfloat16)
    own = direction[...]
    low_own[...] = jnp.concatenate([own[:, :half], own[:, half:]], axis=0).astype(jnp.bfloat16)

    pl.semaphore_wait(
        barrier, nb - jnp.where(mine, 1, 0) + nb - 1 + nc - 1
    )

    def pts_copy(k):
        return pltpu.make_async_remote_copy(
            src_ref=pts_own, dst_ref=pts_buf.at[slot],
            send_sem=pts_send.at[k], recv_sem=pts_recv.at[slot],
            device_id=(k, keeper), device_id_type=MESH,
        )

    def low_copy(k):
        return pltpu.make_async_remote_copy(
            src_ref=low_own, dst_ref=low_buf.at[slot, c],
            send_sem=low_send.at[k], recv_sem=low_recv.at[slot, c],
            device_id=(k, keeper), device_id_type=MESH,
        )

    def each_pts(act):
        def step(k, carry):
            block = c + k * nc

            @pl.when(block != b)
            def _():
                act(pts_copy(block))

            return carry

        lax.fori_loop(0, per, step, 0)

    def each_low(act):
        def step(k, carry):
            block = (b + k) % nb

            @pl.when(jnp.logical_or(k != 0, jnp.logical_not(mine)))
            def _():
                act(low_copy(block))

            return carry

        lax.fori_loop(0, nb, step, 0)

    each_pts(lambda copy: copy.start())
    each_low(lambda copy: copy.start())

    @pl.when(mine)
    def _():
        pts_buf[slot] = pts_own[...]
        low_buf[slot, c] = low_own[...]

    first, second, third = split3(scaled * (-2.0 * KAPPA))
    norms = split3(KAPPA * jnp.sum(scaled * scaled, axis=0, keepdims=True))
    near[0:16, :] = first.astype(jnp.bfloat16)
    near[16:32, :] = second.astype(jnp.bfloat16)
    near[32:48, :] = third.astype(jnp.bfloat16)
    near[48:64, :] = extra_rows((1.0, 1.0, 1.0) + norms, count)

    shift = jnp.log(outscale[...] * (LN2 * LN2 / 3.0)) * LOG2E

    def form(jb):
        @pl.when(base + jb != b)
        def _():
            pltpu.make_async_copy(pts_buf.at[jb], pts_buf.at[jb], pts_recv.at[jb]).wait()

        other = pts_buf[jb]
        wide = other.astype(jnp.float32)
        squares = split3(KAPPA * jnp.sum(wide * wide, axis=0, keepdims=True))
        stacked = jnp.concatenate(
            [other, other, other, extra_rows(squares + (1.0, 1.0, 1.0), count)], axis=0
        )
        far[...] = stacked.T

    def fill(it, kmat):
        cut = slice(it * tile, (it + 1) * tile)
        gap = jnp.dot(far[...], near[:, cut], preferred_element_type=jnp.float32)
        gap = jnp.maximum(gap, 1e-30)
        radius = gap * lax.rsqrt(gap)
        value = ((radius + 3.0 / LN2) * radius + 3.0 / (LN2 * LN2)) * jnp.exp2(shift - radius)
        kmat[:, cut] = value.astype(jnp.bfloat16)

    def wait_low(jb):
        for col in range(nc):
            @pl.when(jnp.logical_or(base + jb != b, c != col))
            def _():
                pltpu.make_async_copy(
                    low_buf.at[jb, col], low_buf.at[jb, col], low_recv.at[jb, col]
                ).wait()

        shards = []
        for col in range(nc):
            wide = low_buf[jb, col].astype(jnp.float32)
            shards.append(jnp.concatenate([wide[:cols], wide[cols:]], axis=1))
        low_all[...] = jnp.concatenate(shards, axis=0).astype(jnp.bfloat16)

    def add_image(it, kmat, first):
        cut = slice(it * tile, (it + 1) * tile)
        total = jnp.dot(low_all[...], kmat[:, cut], preferred_element_type=jnp.float32)
        for col in range(nc):
            rows = total[col * cols : (col + 1) * cols]
            part[col, :, cut] = rows if first else part[col, :, cut] + rows

    def both(jb, now_mat, last_mat, first):
        form(jb)
        wait_low(jb - 1)
        for it in range(tiles):
            fill(it, now_mat)
            add_image(it, last_mat, first)

    form(0)
    for it in range(tiles):
        fill(it, kmat_a)
    both(1, kmat_b, kmat_a, True)

    def pair(p, carry):
        both(2 * p, kmat_a, kmat_b, False)
        both(2 * p + 1, kmat_b, kmat_a, False)
        return carry

    if per > 2:
        lax.fori_loop(1, per // 2, pair, 0)

    def part_copy(it, col):
        cut = pl.ds(pl.multiple_of(it * tile, tile), tile)
        return pltpu.make_async_remote_copy(
            src_ref=part.at[col, :, cut], dst_ref=part_in.at[c, :, cut],
            send_sem=part_send.at[it, col], recv_sem=part_recv.at[it, c],
            device_id=(b, col), device_id_type=MESH,
        )

    wait_low(per - 1)
    for it in range(tiles):
        add_image(it, kmat_b, False)
        for k in range(1, nc):
            part_copy(it, (c + k) % nc).start()

    now = residual[...]
    image = part[c] + noise[...] * own
    for k in range(1, nc):
        col = (c + k) % nc
        for it in range(tiles):
            cut = pl.ds(it * tile, tile)
            pltpu.make_async_copy(
                part_in.at[col, :, cut], part_in.at[col, :, cut], part_recv.at[it, col]
            ).wait()
        image = image + part_in[col]

    lane = lax.broadcasted_iota(jnp.int32, (cols, 128), 1)
    sums = jnp.zeros((cols, 128), jnp.float32)
    for index, product in enumerate((own * image, now * image, image * image, now * now)):
        sums = jnp.where(lane == index, jnp.sum(product, axis=1, keepdims=True), sums)
    stat[...] = sums

    def stat_copy(block):
        return pltpu.make_async_remote_copy(
            src_ref=stat, dst_ref=stat_in.at[b],
            send_sem=stat_send.at[block], recv_sem=stat_recv.at[b],
            device_id=(block, c), device_id_type=MESH,
        )

    def start_stat(k, carry):
        stat_copy((b + k) % nb).start()
        return carry

    lax.fori_loop(1, nb, start_stat, 0)

    def add_stat(k, total):
        block = (b + k) % nb
        pltpu.make_async_copy(stat_in.at[block], stat_in.at[block], stat_recv.at[block]).wait()
        return total + stat_in[block]

    sums = lax.fori_loop(1, nb, add_stat, sums)
    curve, mixed, power, norm_now = (sums[:, index : index + 1] for index in range(4))
    alpha = norm_now / curve
    norm_next = norm_now - 2.0 * alpha * mixed + alpha * alpha * power
    changes[0:cols] = alpha * own
    changes[cols : 2 * cols] = alpha * image
    changes[2 * cols : 3 * cols] = (norm_next / norm_now) * own

    each_pts(lambda copy: copy.wait_send())
    each_low(lambda copy: copy.wait_send())

    def sent_part(k, carry):
        part_copy(k // (nc - 1), (c + 1 + k % (nc - 1)) % nc).wait_send()
        return carry

    lax.fori_loop(0, tiles * (nc - 1), sent_part, 0)

    def sent_stat(k, carry):
        stat_copy((b + k) % nb).wait_send()
        return carry

    lax.fori_loop(1, nb, sent_stat, 0)


def local(nb, nc, points, lengths, noise, outscale, solution, residual, direction):
    dim, count = points.shape
    cols = direction.shape[0]
    per = nb // nc
    tile = math.gcd(count, 256)
    tiles = count // tile
    vmem = pl.BlockSpec(memory_space=pltpu.VMEM)
    here = pl.BlockSpec(memory_space=pl.ANY)
    dma = pltpu.SemaphoreType.DMA
    entries = per * count * count
    changes = pl.pallas_call(
        functools.partial(kernel, nb, nc, tile),
        out_shape=jax.ShapeDtypeStruct((3 * cols, count), jnp.float32),
        in_specs=[here] * 6,
        out_specs=vmem,
        scratch_shapes=[
            pltpu.VMEM((dim, count), jnp.float32),
            pltpu.SMEM((dim,), jnp.float32),
            pltpu.VMEM((1, count), jnp.float32),
            pltpu.VMEM((1, 1), jnp.float32),
            pltpu.VMEM((cols, count), jnp.float32),
            pltpu.VMEM((cols, count), jnp.float32),
            dma((6,)),
            pltpu.VMEM((2 * cols, count // 2), jnp.bfloat16),
            pltpu.VMEM((dim, count), jnp.bfloat16),
            pltpu.VMEM((per, nc, 2 * cols, count // 2), jnp.bfloat16),
            pltpu.VMEM((per, dim, count), jnp.bfloat16),
            pltpu.VMEM((count, DEPTH), jnp.bfloat16),
            pltpu.VMEM((DEPTH, count), jnp.bfloat16),
            pltpu.VMEM((nc * cols, count), jnp.bfloat16),
            pltpu.VMEM((count, count), jnp.bfloat16),
            pltpu.VMEM((count, count), jnp.bfloat16),
            pltpu.VMEM((nc, cols, count), jnp.float32),
            pltpu.VMEM((nc, cols, count), jnp.float32),
            pltpu.VMEM((cols, 128), jnp.float32),
            pltpu.VMEM((nb, cols, 128), jnp.float32),
            dma((nb,)), dma((per, nc)), dma((nb,)), dma((per,)),
            dma((tiles, nc)), dma((tiles, nc)), dma((nb,)), dma((nb,)),
        ],
        compiler_params=pltpu.CompilerParams(
            collective_id=0, has_side_effects=True, vmem_limit_bytes=56 * 1024 * 1024
        ),
        cost_estimate=pl.CostEstimate(
            flops=2 * entries * (DEPTH + nc * cols), bytes_accessed=1 << 19, transcendentals=2 * entries
        ),
    )(points, lengths, noise.reshape(1, count), outscale.reshape(1, 1), residual, direction)
    after = residual - changes[cols : 2 * cols]
    return (solution + changes[:cols], after, after + changes[2 * cols :])


def solution(mesh):
    in_specs = (
        P(None, "blk"), P(), P("blk"), P(),
        P("col", "blk"), P("col", "blk"), P("col", "blk"),
    )
    out_specs = (P("col", "blk"), P("col", "blk"), P("col", "blk"))
    body = functools.partial(local, mesh.shape["blk"], mesh.shape["col"])
    return jax.shard_map(body, mesh=mesh, in_specs=in_specs, out_specs=out_specs, check_vma=False)
```

```python
import functools
import math

import jax
import jax.numpy as jnp
from jax import lax
from jax.experimental import pallas as pl
from jax.experimental.pallas import tpu as pltpu
from jax.sharding import PartitionSpec as P

MESH = pl.DeviceIdType.MESH
LOG2E = math.log2(math.e)
LN2 = math.log(2.0)
KAPPA = 5.0 * LOG2E * LOG2E
DEPTH = 64


def split3(x):
    first = x.astype(jnp.bfloat16).astype(jnp.float32)
    second = (x - first).astype(jnp.bfloat16).astype(jnp.float32)
    third = x - first - second
    return first, second, third


def extra_rows(rows, count):
    row = lax.broadcasted_iota(jnp.int32, (16, count), 0)
    block = jnp.zeros((16, count), jnp.float32)
    for index, value in enumerate(rows):
        block = jnp.where(row == index, value, block)
    return block.astype(jnp.bfloat16)


def kernel(
    nb, nc, tile,
    points_in, lengths_in, noise_in, outscale_in, residual_in, direction_in,
    changes,
    points, lengths, noise, outscale, residual, direction, in_sems,
    low_own, pts_own, low_buf, pts_buf, far, near, low_all, kmat_a, kmat_b, part, part_in, stat, stat_in,
    low_send, low_recv, pts_send, pts_recv, part_send, part_recv, stat_send, stat_recv,
):
    b = lax.axis_index("blk")
    c = lax.axis_index("col")
    per = nb // nc
    dim, count = points.shape
    cols = direction.shape[0]
    half = count // 2
    tiles = count // tile
    keeper = b // per
    base = c * per
    slot = b % per
    mine = keeper == c

    loads = [
        pltpu.make_async_copy(source, target, in_sems.at[index])
        for index, (source, target) in enumerate(
            (
                (points_in, points), (lengths_in, lengths), (direction_in, direction),
                (noise_in, noise), (outscale_in, outscale), (residual_in, residual),
            )
        )
    ]
    for load in loads:
        load.start()

    barrier = pltpu.get_barrier_semaphore()

    def greet(block, col):
        pl.semaphore_signal(barrier, inc=1, device_id=(block, col), device_id_type=MESH)

    def greet_sources(k, carry):
        block = base + k // nc
        col = k % nc

        @pl.when(jnp.logical_or(block != b, col != c))
        def _():
            greet(block, col)

        return carry

    lax.fori_loop(0, per * nc, greet_sources, 0)

    def greet_blocks(k, carry):
        greet((b + k) % nb, c)
        return carry

    lax.fori_loop(1, nb, greet_blocks, 0)
    for k in range(1, nc):
        greet(b, (c + k) % nc)

    for load in loads:
        load.wait()
    row = lax.broadcasted_iota(jnp.int32, (dim, 128), 0)
    scale = jnp.zeros((dim, 128), jnp.float32)
    for k in range(dim):
        scale = jnp.where(row == k, lengths[k], scale)
    scaled = points[...] / scale[:, :1]
    pts_own[...] = scaled.astype(jnp.bfloat16)
    own = direction[...]
    low_own[...] = jnp.concatenate([own[:, :half], own[:, half:]], axis=0).astype(jnp.bfloat16)

    pl.semaphore_wait(
        barrier, nb - jnp.where(mine, 1, 0) + nb - 1 + nc - 1
    )

    def pts_copy(k):
        return pltpu.make_async_remote_copy(
            src_ref=pts_own, dst_ref=pts_buf.at[slot],
            send_sem=pts_send.at[k], recv_sem=pts_recv.at[slot],
            device_id=(k, keeper), device_id_type=MESH,
        )

    def low_copy(k):
        return pltpu.make_async_remote_copy(
            src_ref=low_own, dst_ref=low_buf.at[slot, c],
            send_sem=low_send.at[k], recv_sem=low_recv.at[slot, c],
            device_id=(k, keeper), device_id_type=MESH,
        )

    def each_pts(act):
        def step(k, carry):
            block = c + k * nc

            @pl.when(block != b)
            def _():
                act(pts_copy(block))

            return carry

        lax.fori_loop(0, per, step, 0)

    def each_low(act):
        def step(k, carry):
            block = (b + k) % nb

            @pl.when(jnp.logical_or(k != 0, jnp.logical_not(mine)))
            def _():
                act(low_copy(block))

            return carry

        lax.fori_loop(0, nb, step, 0)

    each_pts(lambda copy: copy.start())
    each_low(lambda copy: copy.start())

    @pl.when(mine)
    def _():
        pts_buf[slot] = pts_own[...]
        low_buf[slot, c] = low_own[...]

    first, second, third = split3(scaled * (-2.0 * KAPPA))
    norms = split3(KAPPA * jnp.sum(scaled * scaled, axis=0, keepdims=True))
    near[0:16, :] = first.astype(jnp.bfloat16)
    near[16:32, :] = second.astype(jnp.bfloat16)
    near[32:48, :] = third.astype(jnp.bfloat16)
    near[48:64, :] = extra_rows((1.0, 1.0, 1.0) + norms, count)

    shift = jnp.log(outscale[...] * (LN2 * LN2 / 3.0)) * LOG2E

    def form(jb):
        @pl.when(base + jb != b)
        def _():
            pltpu.make_async_copy(pts_buf.at[jb], pts_buf.at[jb], pts_recv.at[jb]).wait()

        other = pts_buf[jb]
        wide = other.astype(jnp.float32)
        squares = split3(KAPPA * jnp.sum(wide * wide, axis=0, keepdims=True))
        stacked = jnp.concatenate(
            [other, other, other, extra_rows(squares + (1.0, 1.0, 1.0), count)], axis=0
        )
        far[...] = stacked.T

    piece = math.gcd(count, 64)

    def fill(it, kmat):
        cut = slice(it * tile, (it + 1) * tile)
        for start in range(0, count, piece):
            gap = jnp.dot(
                far[start : start + piece], near[:, cut], preferred_element_type=jnp.float32
            )
            gap = jnp.maximum(gap, 1e-30)
            radius = gap * lax.rsqrt(gap)
            value = ((radius + 3.0 / LN2) * radius + 3.0 / (LN2 * LN2)) * jnp.exp2(shift - radius)
            kmat[start : start + piece, cut] = value.astype(jnp.bfloat16)

    def wait_low(jb):
        for col in range(nc):
            @pl.when(jnp.logical_or(base + jb != b, c != col))
            def _():
                pltpu.make_async_copy(
                    low_buf.at[jb, col], low_buf.at[jb, col], low_recv.at[jb, col]
                ).wait()

        shards = []
        for col in range(nc):
            wide = low_buf[jb, col].astype(jnp.float32)
            shards.append(jnp.concatenate([wide[:cols], wide[cols:]], axis=1))
        low_all[...] = jnp.concatenate(shards, axis=0).astype(jnp.bfloat16)

    def add_image(it, kmat, first):
        cut = slice(it * tile, (it + 1) * tile)
        total = jnp.dot(low_all[...], kmat[:, cut], preferred_element_type=jnp.float32)
        for col in range(nc):
            rows = total[col * cols : (col + 1) * cols]
            part[col, :, cut] = rows if first else part[col, :, cut] + rows

    def both(jb, now_mat, last_mat, first):
        form(jb)
        wait_low(jb - 1)
        for it in range(tiles):
            fill(it, now_mat)
            add_image(it, last_mat, first)

    form(0)
    for it in range(tiles):
        fill(it, kmat_a)
    both(1, kmat_b, kmat_a, True)

    def pair(p, carry):
        both(2 * p, kmat_a, kmat_b, False)
        both(2 * p + 1, kmat_b, kmat_a, False)
        return carry

    if per > 2:
        lax.fori_loop(1, per // 2, pair, 0)

    def part_copy(it, col):
        cut = pl.ds(pl.multiple_of(it * tile, tile), tile)
        return pltpu.make_async_remote_copy(
            src_ref=part.at[col, :, cut], dst_ref=part_in.at[c, :, cut],
            send_sem=part_send.at[it, col], recv_sem=part_recv.at[it, c],
            device_id=(b, col), device_id_type=MESH,
        )

    wait_low(per - 1)
    for it in range(tiles):
        add_image(it, kmat_b, False)
        for k in range(1, nc):
            part_copy(it, (c + k) % nc).start()

    now = residual[...]
    image = part[c] + noise[...] * own
    for k in range(1, nc):
        col = (c + k) % nc
        for it in range(tiles):
            cut = pl.ds(it * tile, tile)
            pltpu.make_async_copy(
                part_in.at[col, :, cut], part_in.at[col, :, cut], part_recv.at[it, col]
            ).wait()
        image = image + part_in[col]

    lane = lax.broadcasted_iota(jnp.int32, (cols, 128), 1)
    sums = jnp.zeros((cols, 128), jnp.float32)
    for index, product in enumerate((own * image, now * image, image * image, now * now)):
        sums = jnp.where(lane == index, jnp.sum(product, axis=1, keepdims=True), sums)
    stat[...] = sums

    def stat_copy(block):
        return pltpu.make_async_remote_copy(
            src_ref=stat, dst_ref=stat_in.at[b],
            send_sem=stat_send.at[block], recv_sem=stat_recv.at[b],
            device_id=(block, c), device_id_type=MESH,
        )

    def start_stat(k, carry):
        stat_copy((b + k) % nb).start()
        return carry

    lax.fori_loop(1, nb, start_stat, 0)

    def add_stat(k, total):
        block = (b + k) % nb
        pltpu.make_async_copy(stat_in.at[block], stat_in.at[block], stat_recv.at[block]).wait()
        return total + stat_in[block]

    sums = lax.fori_loop(1, nb, add_stat, sums)
    curve, mixed, power, norm_now = (sums[:, index : index + 1] for index in range(4))
    alpha = norm_now / curve
    norm_next = norm_now - 2.0 * alpha * mixed + alpha * alpha * power
    changes[0:cols] = alpha * own
    changes[cols : 2 * cols] = alpha * image
    changes[2 * cols : 3 * cols] = (norm_next / norm_now) * own

    each_pts(lambda copy: copy.wait_send())
    each_low(lambda copy: copy.wait_send())

    def sent_part(k, carry):
        part_copy(k // (nc - 1), (c + 1 + k % (nc - 1)) % nc).wait_send()
        return carry

    lax.fori_loop(0, tiles * (nc - 1), sent_part, 0)

    def sent_stat(k, carry):
        stat_copy((b + k) % nb).wait_send()
        return carry

    lax.fori_loop(1, nb, sent_stat, 0)


def local(nb, nc, points, lengths, noise, outscale, solution, residual, direction):
    dim, count = points.shape
    cols = direction.shape[0]
    per = nb // nc
    tile = math.gcd(count, 256)
    tiles = count // tile
    vmem = pl.BlockSpec(memory_space=pltpu.VMEM)
    here = pl.BlockSpec(memory_space=pl.ANY)
    dma = pltpu.SemaphoreType.DMA
    entries = per * count * count
    changes = pl.pallas_call(
        functools.partial(kernel, nb, nc, tile),
        out_shape=jax.ShapeDtypeStruct((3 * cols, count), jnp.float32),
        in_specs=[here] * 6,
        out_specs=vmem,
        scratch_shapes=[
            pltpu.VMEM((dim, count), jnp.float32),
            pltpu.SMEM((dim,), jnp.float32),
            pltpu.VMEM((1, count), jnp.float32),
            pltpu.VMEM((1, 1), jnp.float32),
            pltpu.VMEM((cols, count), jnp.float32),
            pltpu.VMEM((cols, count), jnp.float32),
            dma((6,)),
            pltpu.VMEM((2 * cols, count // 2), jnp.bfloat16),
            pltpu.VMEM((dim, count), jnp.bfloat16),
            pltpu.VMEM((per, nc, 2 * cols, count // 2), jnp.bfloat16),
            pltpu.VMEM((per, dim, count), jnp.bfloat16),
            pltpu.VMEM((count, DEPTH), jnp.bfloat16),
            pltpu.VMEM((DEPTH, count), jnp.bfloat16),
            pltpu.VMEM((nc * cols, count), jnp.bfloat16),
            pltpu.VMEM((count, count), jnp.bfloat16),
            pltpu.VMEM((count, count), jnp.bfloat16),
            pltpu.VMEM((nc, cols, count), jnp.float32),
            pltpu.VMEM((nc, cols, count), jnp.float32),
            pltpu.VMEM((cols, 128), jnp.float32),
            pltpu.VMEM((nb, cols, 128), jnp.float32),
            dma((nb,)), dma((per, nc)), dma((nb,)), dma((per,)),
            dma((tiles, nc)), dma((tiles, nc)), dma((nb,)), dma((nb,)),
        ],
        compiler_params=pltpu.CompilerParams(
            collective_id=0, has_side_effects=True, vmem_limit_bytes=56 * 1024 * 1024
        ),
        cost_estimate=pl.CostEstimate(
            flops=2 * entries * (DEPTH + nc * cols), bytes_accessed=1 << 19, transcendentals=2 * entries
        ),
    )(points, lengths, noise.reshape(1, count), outscale.reshape(1, 1), residual, direction)
    after = residual - changes[cols : 2 * cols]
    return (solution + changes[:cols], after, after + changes[2 * cols :])


def solution(mesh):
    in_specs = (
        P(None, "blk"), P(), P("blk"), P(),
        P("col", "blk"), P("col", "blk"), P("col", "blk"),
    )
    out_specs = (P("col", "blk"), P("col", "blk"), P("col", "blk"))
    body = functools.partial(local, mesh.shape["blk"], mesh.shape["col"])
    return jax.shard_map(body, mesh=mesh, in_specs=in_specs, out_specs=out_specs, check_vma=False)
```

```python
import functools
import math

import jax
import jax.numpy as jnp
from jax import lax
from jax.experimental import pallas as pl
from jax.experimental.pallas import tpu as pltpu
from jax.sharding import PartitionSpec as P

MESH = pl.DeviceIdType.MESH
LOG2E = math.log2(math.e)
LN2 = math.log(2.0)
KAPPA = 5.0 * LOG2E * LOG2E
DEPTH = 64


def split3(x):
    first = x.astype(jnp.bfloat16).astype(jnp.float32)
    second = (x - first).astype(jnp.bfloat16).astype(jnp.float32)
    third = x - first - second
    return first, second, third


def repeat(low, high, step):
    if high - low <= 8:
        for index in range(low, high):
            step(index, 0)
    else:
        lax.fori_loop(low, high, step, 0)


def extra_rows(rows, count):
    row = lax.broadcasted_iota(jnp.int32, (16, count), 0)
    block = jnp.zeros((16, count), jnp.float32)
    for index, value in enumerate(rows):
        block = jnp.where(row == index, value, block)
    return block.astype(jnp.bfloat16)


def kernel(
    nb, nc, tile,
    points_in, lengths_in, noise_in, outscale_in, residual_in, direction_in,
    changes,
    points, lengths, noise, outscale, residual, direction, in_sems,
    low_own, pts_own, low_buf, pts_buf, far, near, low_all, kmat_a, kmat_b, part, part_in, stat, stat_in,
    low_send, low_recv, pts_send, pts_recv, part_send, part_recv, stat_send, stat_recv,
):
    b = lax.axis_index("blk")
    c = lax.axis_index("col")
    per = nb // nc
    dim, count = points.shape
    cols = direction.shape[0]
    half = count // 2
    tiles = count // tile
    keeper = b // per
    base = c * per
    slot = b % per
    mine = keeper == c

    loads = [
        pltpu.make_async_copy(source, target, in_sems.at[index])
        for index, (source, target) in enumerate(
            (
                (points_in, points), (lengths_in, lengths), (direction_in, direction),
                (noise_in, noise), (outscale_in, outscale), (residual_in, residual),
            )
        )
    ]
    barrier = pltpu.get_barrier_semaphore()

    def greet(block, col):
        pl.semaphore_signal(barrier, inc=1, device_id=(block, col), device_id_type=MESH)

    def greet_sources(k, carry):
        block = base + k // nc
        col = k % nc

        @pl.when(jnp.logical_or(block != b, col != c))
        def _():
            greet(block, col)

        return carry

    repeat(0, per * nc, greet_sources)

    for k in range(1, nc):
        greet(b, (c + k) % nc)
    for load in loads:
        load.start()

    for load in loads:
        load.wait()
    row = lax.broadcasted_iota(jnp.int32, (dim, 128), 0)
    scale = jnp.zeros((dim, 128), jnp.float32)
    for k in range(dim):
        scale = jnp.where(row == k, lengths[k], scale)
    scaled = points[...] / scale[:, :1]
    pts_own[...] = scaled.astype(jnp.bfloat16)
    own = direction[...]
    low_own[...] = jnp.concatenate([own[:, :half], own[:, half:]], axis=0).astype(jnp.bfloat16)

    pl.semaphore_wait(
        barrier, nb - jnp.where(mine, 1, 0) + nc - 1
    )

    def pts_copy(k):
        return pltpu.make_async_remote_copy(
            src_ref=pts_own, dst_ref=pts_buf.at[slot],
            send_sem=pts_send.at[k], recv_sem=pts_recv.at[slot],
            device_id=(k, keeper), device_id_type=MESH,
        )

    def low_copy(k):
        return pltpu.make_async_remote_copy(
            src_ref=low_own, dst_ref=low_buf.at[slot, c],
            send_sem=low_send.at[k], recv_sem=low_recv.at[slot, c],
            device_id=(k, keeper), device_id_type=MESH,
        )

    def each_pts(act):
        def step(k, carry):
            block = c + k * nc

            @pl.when(block != b)
            def _():
                act(pts_copy(block))

            return carry

        repeat(0, per, step)

    def each_low(act):
        def step(k, carry):
            block = (b + k) % nb

            @pl.when(jnp.logical_or(k != 0, jnp.logical_not(mine)))
            def _():
                act(low_copy(block))

            return carry

        repeat(0, nb, step)

    each_pts(lambda copy: copy.start())
    each_low(lambda copy: copy.start())

    @pl.when(mine)
    def _():
        pts_buf[slot] = pts_own[...]
        low_buf[slot, c] = low_own[...]

    first, second, third = split3(scaled * (-2.0 * KAPPA))
    norms = split3(KAPPA * jnp.sum(scaled * scaled, axis=0, keepdims=True))
    near[0:16, :] = first.astype(jnp.bfloat16)
    near[16:32, :] = second.astype(jnp.bfloat16)
    near[32:48, :] = third.astype(jnp.bfloat16)
    near[48:64, :] = extra_rows((1.0, 1.0, 1.0) + norms, count)

    shift = jnp.log(outscale[...] * (LN2 * LN2 / 3.0)) * LOG2E

    def form(jb):
        @pl.when(base + jb != b)
        def _():
            pltpu.make_async_copy(pts_buf.at[jb], pts_buf.at[jb], pts_recv.at[jb]).wait()

        other = pts_buf[jb]
        wide = other.astype(jnp.float32)
        squares = split3(KAPPA * jnp.sum(wide * wide, axis=0, keepdims=True))
        stacked = jnp.concatenate(
            [other, other, other, extra_rows(squares + (1.0, 1.0, 1.0), count)], axis=0
        )
        far[...] = stacked.T

    piece = math.gcd(count, 64)

    def fill(it, kmat):
        cut = slice(it * tile, (it + 1) * tile)
        for start in range(0, count, piece):
            gap = jnp.dot(
                far[start : start + piece], near[:, cut], preferred_element_type=jnp.float32
            )
            gap = jnp.maximum(gap, 1e-30)
            radius = gap * lax.rsqrt(gap)
            value = ((radius + 3.0 / LN2) * radius + 3.0 / (LN2 * LN2)) * jnp.exp2(shift - radius)
            kmat[start : start + piece, cut] = value.astype(jnp.bfloat16)

    def wait_low(jb):
        for col in range(nc):
            @pl.when(jnp.logical_or(base + jb != b, c != col))
            def _():
                pltpu.make_async_copy(
                    low_buf.at[jb, col], low_buf.at[jb, col], low_recv.at[jb, col]
                ).wait()

        shards = []
        for col in range(nc):
            wide = low_buf[jb, col].astype(jnp.float32)
            shards.append(jnp.concatenate([wide[:cols], wide[cols:]], axis=1))
        low_all[...] = jnp.concatenate(shards, axis=0).astype(jnp.bfloat16)

    def add_image(it, kmat, first):
        cut = slice(it * tile, (it + 1) * tile)
        total = jnp.dot(low_all[...], kmat[:, cut], preferred_element_type=jnp.float32)
        for col in range(nc):
            rows = total[col * cols : (col + 1) * cols]
            part[col, :, cut] = rows if first else part[col, :, cut] + rows

    def both(jb, now_mat, last_mat, first):
        form(jb)
        wait_low(jb - 1)
        for it in range(tiles):
            fill(it, now_mat)
            add_image(it, last_mat, first)

    form(0)
    for it in range(tiles):
        fill(it, kmat_a)
    both(1, kmat_b, kmat_a, True)

    def pair(p, carry):
        both(2 * p, kmat_a, kmat_b, False)
        both(2 * p + 1, kmat_b, kmat_a, False)
        return carry

    if per > 2:
        lax.fori_loop(1, per // 2, pair, 0)

    def part_copy(col, start, width):
        cut = pl.ds(start, width)
        return pltpu.make_async_remote_copy(
            src_ref=part.at[col, :, cut], dst_ref=part_in.at[c, :, cut],
            send_sem=part_send.at[col], recv_sem=part_recv.at[c],
            device_id=(b, col), device_id_type=MESH,
        )

    wait_low(per - 1)
    for it in range(tiles):
        add_image(it, kmat_b, False)
        if it % 2 == 1:
            for k in range(1, nc):
                part_copy((c + k) % nc, (it - 1) * tile, 2 * tile).start()

    each_pts(lambda copy: copy.wait_send())
    each_low(lambda copy: copy.wait_send())
    now = residual[...]
    image = part[c] + noise[...] * own
    for k in range(1, nc):
        col = (c + k) % nc
        pltpu.make_async_copy(part_in.at[col], part_in.at[col], part_recv.at[col]).wait()
        image = image + part_in[col]

    lane = lax.broadcasted_iota(jnp.int32, (cols, 128), 1)
    sums = jnp.zeros((cols, 128), jnp.float32)
    for index, product in enumerate((own * image, now * image, image * image, now * now)):
        sums = jnp.where(lane == index, jnp.sum(product, axis=1, keepdims=True), sums)
    stat[...] = sums

    def stat_copy(block):
        return pltpu.make_async_remote_copy(
            src_ref=stat, dst_ref=stat_in.at[b],
            send_sem=stat_send.at[block], recv_sem=stat_recv.at[b],
            device_id=(block, c), device_id_type=MESH,
        )

    def start_stat(k, carry):
        stat_copy((b + k) % nb).start()
        return carry

    repeat(1, nb, start_stat)

    for k in range(1, nc):
        part_copy((c + k) % nc, 0, count).wait_send()

    def add_stat(k, total):
        block = (b + k) % nb
        pltpu.make_async_copy(stat_in.at[block], stat_in.at[block], stat_recv.at[block]).wait()
        return total + stat_in[block]

    sums = lax.fori_loop(1, nb, add_stat, sums)
    curve, mixed, power, norm_now = (sums[:, index : index + 1] for index in range(4))
    alpha = norm_now / curve
    norm_next = norm_now - 2.0 * alpha * mixed + alpha * alpha * power
    changes[0:cols] = alpha * own
    changes[cols : 2 * cols] = alpha * image
    changes[2 * cols : 3 * cols] = (norm_next / norm_now) * own

    def sent_stat(k, carry):
        stat_copy((b + k) % nb).wait_send()
        return carry

    repeat(1, nb, sent_stat)


def local(nb, nc, points, lengths, noise, outscale, solution, residual, direction):
    dim, count = points.shape
    cols = direction.shape[0]
    per = nb // nc
    tile = math.gcd(count, 256)
    tiles = count // tile
    vmem = pl.BlockSpec(memory_space=pltpu.VMEM)
    here = pl.BlockSpec(memory_space=pl.ANY)
    dma = pltpu.SemaphoreType.DMA
    entries = per * count * count
    changes = pl.pallas_call(
        functools.partial(kernel, nb, nc, tile),
        out_shape=jax.ShapeDtypeStruct((3 * cols, count), jnp.float32),
        in_specs=[here] * 6,
        out_specs=vmem,
        scratch_shapes=[
            pltpu.VMEM((dim, count), jnp.float32),
            pltpu.SMEM((dim,), jnp.float32),
            pltpu.VMEM((1, count), jnp.float32),
            pltpu.VMEM((1, 1), jnp.float32),
            pltpu.VMEM((cols, count), jnp.float32),
            pltpu.VMEM((cols, count), jnp.float32),
            dma((6,)),
            pltpu.VMEM((2 * cols, count // 2), jnp.bfloat16),
            pltpu.VMEM((dim, count), jnp.bfloat16),
            pltpu.VMEM((per, nc, 2 * cols, count // 2), jnp.bfloat16),
            pltpu.VMEM((per, dim, count), jnp.bfloat16),
            pltpu.VMEM((count, DEPTH), jnp.bfloat16),
            pltpu.VMEM((DEPTH, count), jnp.bfloat16),
            pltpu.VMEM((nc * cols, count), jnp.bfloat16),
            pltpu.VMEM((count, count), jnp.bfloat16),
            pltpu.VMEM((count, count), jnp.bfloat16),
            pltpu.VMEM((nc, cols, count), jnp.float32),
            pltpu.VMEM((nc, cols, count), jnp.float32),
            pltpu.VMEM((cols, 128), jnp.float32),
            pltpu.VMEM((nb, cols, 128), jnp.float32),
            dma((nb,)), dma((per, nc)), dma((nb,)), dma((per,)),
            dma((nc,)), dma((nc,)), dma((nb,)), dma((nb,)),
        ],
        compiler_params=pltpu.CompilerParams(
            collective_id=0, has_side_effects=True, vmem_limit_bytes=56 * 1024 * 1024
        ),
        cost_estimate=pl.CostEstimate(
            flops=2 * entries * (DEPTH + nc * cols), bytes_accessed=1 << 19, transcendentals=2 * entries
        ),
    )(points, lengths, noise.reshape(1, count), outscale.reshape(1, 1), residual, direction)
    after = residual - changes[cols : 2 * cols]
    return (solution + changes[:cols], after, after + changes[2 * cols :])


def solution(mesh):
    in_specs = (
        P(None, "blk"), P(), P("blk"), P(),
        P("col", "blk"), P("col", "blk"), P("col", "blk"),
    )
    out_specs = (P("col", "blk"), P("col", "blk"), P("col", "blk"))
    body = functools.partial(local, mesh.shape["blk"], mesh.shape["col"])
    return jax.shard_map(body, mesh=mesh, in_specs=in_specs, out_specs=out_specs, check_vma=False)
```

```python
import functools
import math

import jax
import jax.numpy as jnp
from jax import lax
from jax.experimental import pallas as pl
from jax.experimental.pallas import tpu as pltpu
from jax.sharding import PartitionSpec as P

MESH = pl.DeviceIdType.MESH
LOG2E = math.log2(math.e)
LN2 = math.log(2.0)
KAPPA = 5.0 * LOG2E * LOG2E
DEPTH = 64


def split3(x):
    first = x.astype(jnp.bfloat16).astype(jnp.float32)
    second = (x - first).astype(jnp.bfloat16).astype(jnp.float32)
    third = x - first - second
    return first, second, third


def repeat(low, high, step):
    if high - low <= 8:
        for index in range(low, high):
            step(index, 0)
    else:
        lax.fori_loop(low, high, step, 0)


def extra_rows(rows, count):
    row = lax.broadcasted_iota(jnp.int32, (16, count), 0)
    block = jnp.zeros((16, count), jnp.float32)
    for index, value in enumerate(rows):
        block = jnp.where(row == index, value, block)
    return block.astype(jnp.bfloat16)


def kernel(
    nb, nc, tile,
    points_in, lengths_in, noise_in, outscale_in, residual_in, direction_in,
    changes,
    points, lengths, noise, outscale, residual, direction, in_sems,
    low_own, pts_own, low_buf, pts_buf, far, near, low_all, kmat_a, kmat_b, part, part_in, stat, stat_in,
    low_send, low_recv, pts_send, pts_recv, part_send, part_recv, stat_send, stat_recv,
):
    b = lax.axis_index("blk")
    c = lax.axis_index("col")
    per = nb // nc
    dim, count = points.shape
    cols = direction.shape[0]
    half = count // 2
    tiles = count // tile
    keeper = b // per
    base = c * per
    slot = b % per
    mine = keeper == c

    loads = [
        pltpu.make_async_copy(source, target, in_sems.at[index])
        for index, (source, target) in enumerate(
            (
                (points_in, points), (lengths_in, lengths), (direction_in, direction),
                (noise_in, noise), (outscale_in, outscale), (residual_in, residual),
            )
        )
    ]
    barrier = pltpu.get_barrier_semaphore()

    def greet(block, col):
        pl.semaphore_signal(barrier, inc=1, device_id=(block, col), device_id_type=MESH)

    def greet_sources(k, carry):
        block = base + k // nc
        col = k % nc

        @pl.when(jnp.logical_or(block != b, col != c))
        def _():
            greet(block, col)

        return carry

    repeat(0, per * nc, greet_sources)

    for k in range(1, nc):
        greet(b, (c + k) % nc)
    for load in loads:
        load.start()

    for load in loads:
        load.wait()
    row = lax.broadcasted_iota(jnp.int32, (dim, 128), 0)
    scale = jnp.zeros((dim, 128), jnp.float32)
    for k in range(dim):
        scale = jnp.where(row == k, lengths[k], scale)
    scaled = points[...] / scale[:, :1]
    pts_own[...] = scaled.astype(jnp.bfloat16)
    own = direction[...]
    low_own[...] = jnp.concatenate([own[:, :half], own[:, half:]], axis=0).astype(jnp.bfloat16)

    pl.semaphore_wait(
        barrier, nb - jnp.where(mine, 1, 0) + nc - 1
    )

    def pts_copy(k):
        return pltpu.make_async_remote_copy(
            src_ref=pts_own, dst_ref=pts_buf.at[slot],
            send_sem=pts_send.at[k], recv_sem=pts_recv.at[slot],
            device_id=(k, keeper), device_id_type=MESH,
        )

    def low_copy(k):
        return pltpu.make_async_remote_copy(
            src_ref=low_own, dst_ref=low_buf.at[slot, c],
            send_sem=low_send.at[k], recv_sem=low_recv.at[slot, c],
            device_id=(k, keeper), device_id_type=MESH,
        )

    def each_pts(act):
        def step(k, carry):
            block = c + k * nc

            @pl.when(block != b)
            def _():
                act(pts_copy(block))

            return carry

        repeat(0, per, step)

    def each_low(act):
        def step(k, carry):
            block = (b + k) % nb

            @pl.when(jnp.logical_or(k != 0, jnp.logical_not(mine)))
            def _():
                act(low_copy(block))

            return carry

        repeat(0, nb, step)

    each_pts(lambda copy: copy.start())

    @pl.when(mine)
    def _():
        pts_buf[slot] = pts_own[...]
        low_buf[slot, c] = low_own[...]

    first, second, third = split3(scaled * (-2.0 * KAPPA))
    norms = split3(KAPPA * jnp.sum(scaled * scaled, axis=0, keepdims=True))
    near[0:16, :] = first.astype(jnp.bfloat16)
    near[16:32, :] = second.astype(jnp.bfloat16)
    near[32:48, :] = third.astype(jnp.bfloat16)
    near[48:64, :] = extra_rows((1.0, 1.0, 1.0) + norms, count)

    shift = jnp.log(outscale[...] * (LN2 * LN2 / 3.0)) * LOG2E

    def wait_pts(jb):
        @pl.when(base + jb != b)
        def _():
            pltpu.make_async_copy(pts_buf.at[jb], pts_buf.at[jb], pts_recv.at[jb]).wait()

    def form(jb):
        other = pts_buf[jb]
        wide = other.astype(jnp.float32)
        squares = split3(KAPPA * jnp.sum(wide * wide, axis=0, keepdims=True))
        stacked = jnp.concatenate(
            [other, other, other, extra_rows(squares + (1.0, 1.0, 1.0), count)], axis=0
        )
        far[...] = stacked.T

    piece = math.gcd(count, 64)

    def fill(it, kmat):
        cut = slice(it * tile, (it + 1) * tile)
        for start in range(0, count, piece):
            gap = jnp.dot(
                far[start : start + piece], near[:, cut], preferred_element_type=jnp.float32
            )
            gap = jnp.maximum(gap, 1e-30)
            radius = gap * lax.rsqrt(gap)
            value = ((radius + 3.0 / LN2) * radius + 3.0 / (LN2 * LN2)) * jnp.exp2(shift - radius)
            kmat[start : start + piece, cut] = value.astype(jnp.bfloat16)

    def wait_low(jb):
        for col in range(nc):
            @pl.when(jnp.logical_or(base + jb != b, c != col))
            def _():
                pltpu.make_async_copy(
                    low_buf.at[jb, col], low_buf.at[jb, col], low_recv.at[jb, col]
                ).wait()

        shards = []
        for col in range(nc):
            wide = low_buf[jb, col].astype(jnp.float32)
            shards.append(jnp.concatenate([wide[:cols], wide[cols:]], axis=1))
        low_all[...] = jnp.concatenate(shards, axis=0).astype(jnp.bfloat16)

    def add_image(it, kmat, first):
        cut = slice(it * tile, (it + 1) * tile)
        total = jnp.dot(low_all[...], kmat[:, cut], preferred_element_type=jnp.float32)
        for col in range(nc):
            rows = total[col * cols : (col + 1) * cols]
            part[col, :, cut] = rows if first else part[col, :, cut] + rows

    def both(jb, now_mat, last_mat, first):
        wait_pts(jb)
        form(jb)
        wait_low(jb - 1)
        for it in range(tiles):
            fill(it, now_mat)
            add_image(it, last_mat, first)

    wait_pts(0)
    each_low(lambda copy: copy.start())
    form(0)
    for it in range(tiles):
        fill(it, kmat_a)
    both(1, kmat_b, kmat_a, True)

    def pair(p, carry):
        both(2 * p, kmat_a, kmat_b, False)
        both(2 * p + 1, kmat_b, kmat_a, False)
        return carry

    if per > 2:
        lax.fori_loop(1, per // 2, pair, 0)

    def part_copy(col, start, width):
        cut = pl.ds(start, width)
        return pltpu.make_async_remote_copy(
            src_ref=part.at[col, :, cut], dst_ref=part_in.at[c, :, cut],
            send_sem=part_send.at[col], recv_sem=part_recv.at[c],
            device_id=(b, col), device_id_type=MESH,
        )

    wait_low(per - 1)
    for it in range(tiles):
        add_image(it, kmat_b, False)
        if it % 2 == 1:
            for k in range(1, nc):
                part_copy((c + k) % nc, (it - 1) * tile, 2 * tile).start()

    each_pts(lambda copy: copy.wait_send())
    each_low(lambda copy: copy.wait_send())
    now = residual[...]
    image = part[c] + noise[...] * own
    for k in range(1, nc):
        col = (c + k) % nc
        pltpu.make_async_copy(part_in.at[col], part_in.at[col], part_recv.at[col]).wait()
        image = image + part_in[col]

    lane = lax.broadcasted_iota(jnp.int32, (cols, 128), 1)
    sums = jnp.zeros((cols, 128), jnp.float32)
    for index, product in enumerate((own * image, now * image, image * image, now * now)):
        sums = jnp.where(lane == index, jnp.sum(product, axis=1, keepdims=True), sums)
    stat[...] = sums

    def stat_copy(block):
        return pltpu.make_async_remote_copy(
            src_ref=stat, dst_ref=stat_in.at[b],
            send_sem=stat_send.at[block], recv_sem=stat_recv.at[b],
            device_id=(block, c), device_id_type=MESH,
        )

    def start_stat(k, carry):
        stat_copy((b + k) % nb).start()
        return carry

    repeat(1, nb, start_stat)

    for k in range(1, nc):
        part_copy((c + k) % nc, 0, count).wait_send()

    def add_stat(k, total):
        block = (b + k) % nb
        pltpu.make_async_copy(stat_in.at[block], stat_in.at[block], stat_recv.at[block]).wait()
        return total + stat_in[block]

    sums = lax.fori_loop(1, nb, add_stat, sums)
    curve, mixed, power, norm_now = (sums[:, index : index + 1] for index in range(4))
    alpha = norm_now / curve
    norm_next = norm_now - 2.0 * alpha * mixed + alpha * alpha * power
    changes[0:cols] = alpha * own
    changes[cols : 2 * cols] = alpha * image
    changes[2 * cols : 3 * cols] = (norm_next / norm_now) * own

    def sent_stat(k, carry):
        stat_copy((b + k) % nb).wait_send()
        return carry

    repeat(1, nb, sent_stat)


def local(nb, nc, points, lengths, noise, outscale, solution, residual, direction):
    dim, count = points.shape
    cols = direction.shape[0]
    per = nb // nc
    tile = math.gcd(count, 256)
    tiles = count // tile
    vmem = pl.BlockSpec(memory_space=pltpu.VMEM)
    here = pl.BlockSpec(memory_space=pl.ANY)
    dma = pltpu.SemaphoreType.DMA
    entries = per * count * count
    changes = pl.pallas_call(
        functools.partial(kernel, nb, nc, tile),
        out_shape=jax.ShapeDtypeStruct((3 * cols, count), jnp.float32),
        in_specs=[here] * 6,
        out_specs=vmem,
        scratch_shapes=[
            pltpu.VMEM((dim, count), jnp.float32),
            pltpu.SMEM((dim,), jnp.float32),
            pltpu.VMEM((1, count), jnp.float32),
            pltpu.VMEM((1, 1), jnp.float32),
            pltpu.VMEM((cols, count), jnp.float32),
            pltpu.VMEM((cols, count), jnp.float32),
            dma((6,)),
            pltpu.VMEM((2 * cols, count // 2), jnp.bfloat16),
            pltpu.VMEM((dim, count), jnp.bfloat16),
            pltpu.VMEM((per, nc, 2 * cols, count // 2), jnp.bfloat16),
            pltpu.VMEM((per, dim, count), jnp.bfloat16),
            pltpu.VMEM((count, DEPTH), jnp.bfloat16),
            pltpu.VMEM((DEPTH, count), jnp.bfloat16),
            pltpu.VMEM((nc * cols, count), jnp.bfloat16),
            pltpu.VMEM((count, count), jnp.bfloat16),
            pltpu.VMEM((count, count), jnp.bfloat16),
            pltpu.VMEM((nc, cols, count), jnp.float32),
            pltpu.VMEM((nc, cols, count), jnp.float32),
            pltpu.VMEM((cols, 128), jnp.float32),
            pltpu.VMEM((nb, cols, 128), jnp.float32),
            dma((nb,)), dma((per, nc)), dma((nb,)), dma((per,)),
            dma((nc,)), dma((nc,)), dma((nb,)), dma((nb,)),
        ],
        compiler_params=pltpu.CompilerParams(
            collective_id=0, has_side_effects=True, vmem_limit_bytes=56 * 1024 * 1024
        ),
        cost_estimate=pl.CostEstimate(
            flops=2 * entries * (DEPTH + nc * cols), bytes_accessed=1 << 19, transcendentals=2 * entries
        ),
    )(points, lengths, noise.reshape(1, count), outscale.reshape(1, 1), residual, direction)
    after = residual - changes[cols : 2 * cols]
    return (solution + changes[:cols], after, after + changes[2 * cols :])


def solution(mesh):
    in_specs = (
        P(None, "blk"), P(), P("blk"), P(),
        P("col", "blk"), P("col", "blk"), P("col", "blk"),
    )
    out_specs = (P("col", "blk"), P("col", "blk"), P("col", "blk"))
    body = functools.partial(local, mesh.shape["blk"], mesh.shape["col"])
    return jax.shard_map(body, mesh=mesh, in_specs=in_specs, out_specs=out_specs, check_vma=False)
```

```python
import functools
import math

import jax
import jax.numpy as jnp
from jax import lax
from jax.experimental import pallas as pl
from jax.experimental.pallas import tpu as pltpu
from jax.sharding import PartitionSpec as P

MESH = pl.DeviceIdType.MESH
LOG2E = math.log2(math.e)
LN2 = math.log(2.0)
KAPPA = 5.0 * LOG2E * LOG2E
DEPTH = 64


def split3(x):
    first = x.astype(jnp.bfloat16).astype(jnp.float32)
    second = (x - first).astype(jnp.bfloat16).astype(jnp.float32)
    third = x - first - second
    return first, second, third


def repeat(low, high, step):
    if high - low <= 8:
        for index in range(low, high):
            step(index, 0)
    else:
        lax.fori_loop(low, high, step, 0)


def extra_rows(rows, count):
    row = lax.broadcasted_iota(jnp.int32, (16, count), 0)
    block = jnp.zeros((16, count), jnp.float32)
    for index, value in enumerate(rows):
        block = jnp.where(row == index, value, block)
    return block.astype(jnp.bfloat16)


def kernel(
    nb, nc, tile,
    points_in, lengths_in, noise_in, outscale_in, residual_in, direction_in,
    changes,
    points, lengths, noise, outscale, residual, direction, in_sems,
    low_own, pts_own, low_buf, pts_buf, far, near, low_all, kmat_a, kmat_b, part, part_in, stat, stat_in,
    low_send, low_recv, pts_send, pts_recv, part_send, part_recv, stat_send, stat_recv,
):
    b = lax.axis_index("blk")
    c = lax.axis_index("col")
    per = nb // nc
    dim, count = points.shape
    cols = direction.shape[0]
    half = count // 2
    tiles = count // tile
    keeper = b // per
    base = c * per
    slot = b % per
    mine = keeper == c

    loads = [
        pltpu.make_async_copy(source, target, in_sems.at[index])
        for index, (source, target) in enumerate(
            (
                (points_in, points), (lengths_in, lengths), (direction_in, direction),
                (noise_in, noise), (outscale_in, outscale), (residual_in, residual),
            )
        )
    ]
    barrier = pltpu.get_barrier_semaphore()

    def greet(block, col):
        pl.semaphore_signal(barrier, inc=1, device_id=(block, col), device_id_type=MESH)

    def greet_sources(k, carry):
        block = base + k // nc
        col = k % nc

        @pl.when(jnp.logical_or(block != b, col != c))
        def _():
            greet(block, col)

        return carry

    repeat(0, per * nc, greet_sources)

    for k in range(1, nc):
        greet(b, (c + k) % nc)
    for load in loads:
        load.start()

    for load in loads:
        load.wait()
    row = lax.broadcasted_iota(jnp.int32, (dim, 128), 0)
    scale = jnp.zeros((dim, 128), jnp.float32)
    for k in range(dim):
        scale = jnp.where(row == k, lengths[k], scale)
    scaled = points[...] / scale[:, :1]
    pts_own[...] = scaled.astype(jnp.bfloat16)
    own = direction[...]
    low_own[...] = jnp.concatenate([own[:, :half], own[:, half:]], axis=0).astype(jnp.bfloat16)

    pl.semaphore_wait(
        barrier, nb - jnp.where(mine, 1, 0) + nc - 1
    )

    def pts_copy(k):
        return pltpu.make_async_remote_copy(
            src_ref=pts_own, dst_ref=pts_buf.at[slot],
            send_sem=pts_send.at[k], recv_sem=pts_recv.at[slot],
            device_id=(k, keeper), device_id_type=MESH,
        )

    def low_copy(k):
        return pltpu.make_async_remote_copy(
            src_ref=low_own, dst_ref=low_buf.at[slot, c],
            send_sem=low_send.at[k], recv_sem=low_recv.at[slot, c],
            device_id=(k, keeper), device_id_type=MESH,
        )

    def each_pts(act):
        def step(k, carry):
            block = c + k * nc

            @pl.when(block != b)
            def _():
                act(pts_copy(block))

            return carry

        repeat(0, per, step)

    def each_low(act):
        def step(k, carry):
            block = (b + k) % nb

            @pl.when(jnp.logical_or(k != 0, jnp.logical_not(mine)))
            def _():
                act(low_copy(block))

            return carry

        repeat(0, nb, step)

    each_pts(lambda copy: copy.start())
    each_low(lambda copy: copy.start())

    @pl.when(mine)
    def _():
        pts_buf[slot] = pts_own[...]
        low_buf[slot, c] = low_own[...]

    first, second, third = split3(scaled * (-2.0 * KAPPA))
    norms = split3(KAPPA * jnp.sum(scaled * scaled, axis=0, keepdims=True))
    near[0:16, :] = first.astype(jnp.bfloat16)
    near[16:32, :] = second.astype(jnp.bfloat16)
    near[32:48, :] = third.astype(jnp.bfloat16)
    near[48:64, :] = extra_rows((1.0, 1.0, 1.0) + norms, count)

    shift = jnp.log(outscale[...] * (LN2 * LN2 / 3.0)) * LOG2E

    def form(jb):
        @pl.when(base + jb != b)
        def _():
            pltpu.make_async_copy(pts_buf.at[jb], pts_buf.at[jb], pts_recv.at[jb]).wait()

        other = pts_buf[jb]
        wide = other.astype(jnp.float32)
        squares = split3(KAPPA * jnp.sum(wide * wide, axis=0, keepdims=True))
        stacked = jnp.concatenate(
            [other, other, other, extra_rows(squares + (1.0, 1.0, 1.0), count)], axis=0
        )
        far[...] = stacked.T

    piece = math.gcd(count, 64)

    def fill(it, kmat):
        cut = slice(it * tile, (it + 1) * tile)
        for start in range(0, count, piece):
            gap = jnp.dot(
                far[start : start + piece], near[:, cut], preferred_element_type=jnp.float32
            )
            gap = jnp.maximum(gap, 1e-30)
            radius = gap * lax.rsqrt(gap)
            value = ((radius + 3.0 / LN2) * radius + 3.0 / (LN2 * LN2)) * jnp.exp2(shift - radius)
            kmat[start : start + piece, cut] = value.astype(jnp.bfloat16)

    def wait_low(jb, place):
        for col in range(nc):
            @pl.when(jnp.logical_or(base + jb != b, c != col))
            def _():
                pltpu.make_async_copy(
                    low_buf.at[jb, col], low_buf.at[jb, col], low_recv.at[jb, col]
                ).wait()

        shards = []
        for col in range(nc):
            wide = low_buf[jb, col].astype(jnp.float32)
            shards.append(jnp.concatenate([wide[:cols], wide[cols:]], axis=1))
        low_all[place] = jnp.concatenate(shards, axis=0).astype(jnp.bfloat16)

    def add_image(it, kmat, place, first):
        cut = slice(it * tile, (it + 1) * tile)
        total = jnp.dot(low_all[place], kmat[:, cut], preferred_element_type=jnp.float32)
        for col in range(nc):
            rows = total[col * cols : (col + 1) * cols]
            part[col, :, cut] = rows if first else part[col, :, cut] + rows

    mats = (kmat_a, kmat_b)
    for slot_index in range(2):
        form(slot_index)
        for it in range(tiles):
            fill(it, mats[slot_index])

    def pair(p, carry):
        for index in range(2):
            wait_low(2 * p - 2 + index, index)
            form(2 * p + index)
            for it in range(tiles):
                add_image(it, mats[index], index, False)
                fill(it, mats[index])
        return carry

    if per > 2:
        part[...] = jnp.zeros_like(part)
        lax.fori_loop(1, per // 2, pair, 0)

    def part_copy(col, start, width):
        cut = pl.ds(start, width)
        return pltpu.make_async_remote_copy(
            src_ref=part.at[col, :, cut], dst_ref=part_in.at[c, :, cut],
            send_sem=part_send.at[col], recv_sem=part_recv.at[c],
            device_id=(b, col), device_id_type=MESH,
        )

    for index in range(2):
        wait_low(per - 2 + index, index)
    for it in range(tiles):
        for index in range(2):
            add_image(it, mats[index], index, per == 2 and index == 0)
        if it % 2 == 1:
            for k in range(1, nc):
                part_copy((c + k) % nc, (it - 1) * tile, 2 * tile).start()

    each_pts(lambda copy: copy.wait_send())
    each_low(lambda copy: copy.wait_send())
    now = residual[...]
    image = part[c] + noise[...] * own
    for k in range(1, nc):
        col = (c + k) % nc
        pltpu.make_async_copy(part_in.at[col], part_in.at[col], part_recv.at[col]).wait()
        image = image + part_in[col]

    lane = lax.broadcasted_iota(jnp.int32, (cols, 128), 1)
    sums = jnp.zeros((cols, 128), jnp.float32)
    for index, product in enumerate((own * image, now * image, image * image, now * now)):
        sums = jnp.where(lane == index, jnp.sum(product, axis=1, keepdims=True), sums)
    stat[...] = sums

    def stat_copy(block):
        return pltpu.make_async_remote_copy(
            src_ref=stat, dst_ref=stat_in.at[b],
            send_sem=stat_send.at[block], recv_sem=stat_recv.at[b],
            device_id=(block, c), device_id_type=MESH,
        )

    def start_stat(k, carry):
        stat_copy((b + k) % nb).start()
        return carry

    repeat(1, nb, start_stat)

    for k in range(1, nc):
        part_copy((c + k) % nc, 0, count).wait_send()

    def add_stat(k, total):
        block = (b + k) % nb
        pltpu.make_async_copy(stat_in.at[block], stat_in.at[block], stat_recv.at[block]).wait()
        return total + stat_in[block]

    sums = lax.fori_loop(1, nb, add_stat, sums)
    curve, mixed, power, norm_now = (sums[:, index : index + 1] for index in range(4))
    alpha = norm_now / curve
    norm_next = norm_now - 2.0 * alpha * mixed + alpha * alpha * power
    changes[0:cols] = alpha * own
    changes[cols : 2 * cols] = alpha * image
    changes[2 * cols : 3 * cols] = (norm_next / norm_now) * own

    def sent_stat(k, carry):
        stat_copy((b + k) % nb).wait_send()
        return carry

    repeat(1, nb, sent_stat)


def local(nb, nc, points, lengths, noise, outscale, solution, residual, direction):
    dim, count = points.shape
    cols = direction.shape[0]
    per = nb // nc
    tile = math.gcd(count, 256)
    tiles = count // tile
    vmem = pl.BlockSpec(memory_space=pltpu.VMEM)
    here = pl.BlockSpec(memory_space=pl.ANY)
    dma = pltpu.SemaphoreType.DMA
    entries = per * count * count
    changes = pl.pallas_call(
        functools.partial(kernel, nb, nc, tile),
        out_shape=jax.ShapeDtypeStruct((3 * cols, count), jnp.float32),
        in_specs=[here] * 6,
        out_specs=vmem,
        scratch_shapes=[
            pltpu.VMEM((dim, count), jnp.float32),
            pltpu.SMEM((dim,), jnp.float32),
            pltpu.VMEM((1, count), jnp.float32),
            pltpu.VMEM((1, 1), jnp.float32),
            pltpu.VMEM((cols, count), jnp.float32),
            pltpu.VMEM((cols, count), jnp.float32),
            dma((6,)),
            pltpu.VMEM((2 * cols, count // 2), jnp.bfloat16),
            pltpu.VMEM((dim, count), jnp.bfloat16),
            pltpu.VMEM((per, nc, 2 * cols, count // 2), jnp.bfloat16),
            pltpu.VMEM((per, dim, count), jnp.bfloat16),
            pltpu.VMEM((count, DEPTH), jnp.bfloat16),
            pltpu.VMEM((DEPTH, count), jnp.bfloat16),
            pltpu.VMEM((2, nc * cols, count), jnp.bfloat16),
            pltpu.VMEM((count, count), jnp.bfloat16),
            pltpu.VMEM((count, count), jnp.bfloat16),
            pltpu.VMEM((nc, cols, count), jnp.float32),
            pltpu.VMEM((nc, cols, count), jnp.float32),
            pltpu.VMEM((cols, 128), jnp.float32),
            pltpu.VMEM((nb, cols, 128), jnp.float32),
            dma((nb,)), dma((per, nc)), dma((nb,)), dma((per,)),
            dma((nc,)), dma((nc,)), dma((nb,)), dma((nb,)),
        ],
        compiler_params=pltpu.CompilerParams(
            collective_id=0, has_side_effects=True, vmem_limit_bytes=56 * 1024 * 1024
        ),
        cost_estimate=pl.CostEstimate(
            flops=2 * entries * (DEPTH + nc * cols), bytes_accessed=1 << 19, transcendentals=2 * entries
        ),
    )(points, lengths, noise.reshape(1, count), outscale.reshape(1, 1), residual, direction)
    after = residual - changes[cols : 2 * cols]
    return (solution + changes[:cols], after, after + changes[2 * cols :])


def solution(mesh):
    in_specs = (
        P(None, "blk"), P(), P("blk"), P(),
        P("col", "blk"), P("col", "blk"), P("col", "blk"),
    )
    out_specs = (P("col", "blk"), P("col", "blk"), P("col", "blk"))
    body = functools.partial(local, mesh.shape["blk"], mesh.shape["col"])
    return jax.shard_map(body, mesh=mesh, in_specs=in_specs, out_specs=out_specs, check_vma=False)
```

```python
import functools
import math

import jax
import jax.numpy as jnp
from jax import lax
from jax.experimental import pallas as pl
from jax.experimental.pallas import tpu as pltpu
from jax.sharding import PartitionSpec as P

MESH = pl.DeviceIdType.MESH
LOG2E = math.log2(math.e)
LN2 = math.log(2.0)
KAPPA = 5.0 * LOG2E * LOG2E
DEPTH = 64


def split3(x):
    first = x.astype(jnp.bfloat16).astype(jnp.float32)
    second = (x - first).astype(jnp.bfloat16).astype(jnp.float32)
    third = x - first - second
    return first, second, third


def repeat(low, high, step):
    if high - low <= 8:
        for index in range(low, high):
            step(index, 0)
    else:
        lax.fori_loop(low, high, step, 0)


def extra_rows(rows, count):
    row = lax.broadcasted_iota(jnp.int32, (16, count), 0)
    block = jnp.zeros((16, count), jnp.float32)
    for index, value in enumerate(rows):
        block = jnp.where(row == index, value, block)
    return block.astype(jnp.bfloat16)


def kernel(
    nb, nc, tile,
    points_in, lengths_in, noise_in, outscale_in, residual_in, direction_in,
    changes,
    points, lengths, noise, outscale, residual, direction, in_sems,
    low_own, pts_own, low_buf, pts_buf, far, near, low_all, kmat_a, kmat_b, part, part_in, stat, stat_in,
    low_send, low_recv, pts_send, pts_recv, part_send, part_recv, stat_send, stat_recv,
):
    b = lax.axis_index("blk")
    c = lax.axis_index("col")
    per = nb // nc
    dim, count = points.shape
    cols = direction.shape[0]
    half = count // 2
    tiles = count // tile
    keeper = b // per
    base = c * per
    slot = b % per
    mine = keeper == c

    loads = [
        pltpu.make_async_copy(source, target, in_sems.at[index])
        for index, (source, target) in enumerate(
            (
                (points_in, points), (lengths_in, lengths), (direction_in, direction),
                (noise_in, noise), (outscale_in, outscale), (residual_in, residual),
            )
        )
    ]
    barrier = pltpu.get_barrier_semaphore()

    def greet(block, col):
        pl.semaphore_signal(barrier, inc=1, device_id=(block, col), device_id_type=MESH)

    def greet_sources(k, carry):
        block = base + k // nc
        col = k % nc

        @pl.when(jnp.logical_or(block != b, col != c))
        def _():
            greet(block, col)

        return carry

    repeat(0, per * nc, greet_sources)

    for k in range(1, nc):
        greet(b, (c + k) % nc)
    for load in loads:
        load.start()

    for load in loads:
        load.wait()
    row = lax.broadcasted_iota(jnp.int32, (dim, 128), 0)
    scale = jnp.zeros((dim, 128), jnp.float32)
    for k in range(dim):
        scale = jnp.where(row == k, lengths[k], scale)
    scaled = points[...] / scale[:, :1]
    pts_own[...] = scaled.astype(jnp.bfloat16)
    own = direction[...]
    low_own[...] = jnp.concatenate([own[:, :half], own[:, half:]], axis=0).astype(jnp.bfloat16)

    pl.semaphore_wait(
        barrier, nb - jnp.where(mine, 1, 0) + nc - 1
    )

    def pts_copy(k):
        return pltpu.make_async_remote_copy(
            src_ref=pts_own, dst_ref=pts_buf.at[slot],
            send_sem=pts_send.at[k], recv_sem=pts_recv.at[slot],
            device_id=(k, keeper), device_id_type=MESH,
        )

    def low_copy(k):
        return pltpu.make_async_remote_copy(
            src_ref=low_own, dst_ref=low_buf.at[slot, c],
            send_sem=low_send.at[k], recv_sem=low_recv.at[slot, c],
            device_id=(k, keeper), device_id_type=MESH,
        )

    def each_pts(act):
        def step(k, carry):
            block = c + k * nc

            @pl.when(block != b)
            def _():
                act(pts_copy(block))

            return carry

        repeat(0, per, step)

    half_blocks = nb // 2
    side = b // half_blocks

    def each_low(act):
        def step(k, carry):
            other = lax.rem(side + 1 + k // half_blocks, 2)
            block = other * half_blocks + (b + k) % half_blocks

            @pl.when(jnp.logical_or(k != half_blocks, jnp.logical_not(mine)))
            def _():
                act(low_copy(block))

            return carry

        repeat(0, nb, step)

    each_pts(lambda copy: copy.start())
    each_low(lambda copy: copy.start())

    @pl.when(mine)
    def _():
        pts_buf[slot] = pts_own[...]
        low_buf[slot, c] = low_own[...]

    first, second, third = split3(scaled * (-2.0 * KAPPA))
    norms = split3(KAPPA * jnp.sum(scaled * scaled, axis=0, keepdims=True))
    near[0:16, :] = first.astype(jnp.bfloat16)
    near[16:32, :] = second.astype(jnp.bfloat16)
    near[32:48, :] = third.astype(jnp.bfloat16)
    near[48:64, :] = extra_rows((1.0, 1.0, 1.0) + norms, count)

    shift = jnp.log(outscale[...] * (LN2 * LN2 / 3.0)) * LOG2E

    def form(jb):
        @pl.when(base + jb != b)
        def _():
            pltpu.make_async_copy(pts_buf.at[jb], pts_buf.at[jb], pts_recv.at[jb]).wait()

        other = pts_buf[jb]
        wide = other.astype(jnp.float32)
        squares = split3(KAPPA * jnp.sum(wide * wide, axis=0, keepdims=True))
        stacked = jnp.concatenate(
            [other, other, other, extra_rows(squares + (1.0, 1.0, 1.0), count)], axis=0
        )
        far[...] = stacked.T

    piece = math.gcd(count, 64)

    def fill(it, kmat):
        cut = slice(it * tile, (it + 1) * tile)
        for start in range(0, count, piece):
            gap = jnp.dot(
                far[start : start + piece], near[:, cut], preferred_element_type=jnp.float32
            )
            gap = jnp.maximum(gap, 1e-30)
            radius = gap * lax.rsqrt(gap)
            value = ((radius + 3.0 / LN2) * radius + 3.0 / (LN2 * LN2)) * jnp.exp2(shift - radius)
            kmat[start : start + piece, cut] = value.astype(jnp.bfloat16)

    def wait_low(jb, place):
        for col in range(nc):
            @pl.when(jnp.logical_or(base + jb != b, c != col))
            def _():
                pltpu.make_async_copy(
                    low_buf.at[jb, col], low_buf.at[jb, col], low_recv.at[jb, col]
                ).wait()

        shards = []
        for col in range(nc):
            wide = low_buf[jb, col].astype(jnp.float32)
            shards.append(jnp.concatenate([wide[:cols], wide[cols:]], axis=1))
        low_all[place] = jnp.concatenate(shards, axis=0).astype(jnp.bfloat16)

    def add_image(it, kmat, place, first):
        cut = slice(it * tile, (it + 1) * tile)
        total = jnp.dot(low_all[place], kmat[:, cut], preferred_element_type=jnp.float32)
        for col in range(nc):
            rows = total[col * cols : (col + 1) * cols]
            part[col, :, cut] = rows if first else part[col, :, cut] + rows

    mats = (kmat_a, kmat_b)
    for slot_index in range(2):
        form(slot_index)
        for it in range(tiles):
            fill(it, mats[slot_index])

    def pair(p, carry):
        for index in range(2):
            wait_low(2 * p - 2 + index, index)
            form(2 * p + index)
            for it in range(tiles):
                add_image(it, mats[index], index, False)
                fill(it, mats[index])
        return carry

    if per > 2:
        part[...] = jnp.zeros_like(part)
        lax.fori_loop(1, per // 2, pair, 0)

    def part_copy(col, start, width):
        cut = pl.ds(start, width)
        return pltpu.make_async_remote_copy(
            src_ref=part.at[col, :, cut], dst_ref=part_in.at[c, :, cut],
            send_sem=part_send.at[col], recv_sem=part_recv.at[c],
            device_id=(b, col), device_id_type=MESH,
        )

    for index in range(2):
        wait_low(per - 2 + index, index)
    for it in range(tiles):
        for index in range(2):
            add_image(it, mats[index], index, per == 2 and index == 0)
        if it % 2 == 1:
            for k in range(1, nc):
                part_copy((c + k) % nc, (it - 1) * tile, 2 * tile).start()

    each_pts(lambda copy: copy.wait_send())
    each_low(lambda copy: copy.wait_send())
    now = residual[...]
    image = part[c] + noise[...] * own
    for k in range(1, nc):
        col = (c + k) % nc
        pltpu.make_async_copy(part_in.at[col], part_in.at[col], part_recv.at[col]).wait()
        image = image + part_in[col]

    lane = lax.broadcasted_iota(jnp.int32, (cols, 128), 1)
    sums = jnp.zeros((cols, 128), jnp.float32)
    for index, product in enumerate((own * image, now * image, image * image, now * now)):
        sums = jnp.where(lane == index, jnp.sum(product, axis=1, keepdims=True), sums)
    stat[...] = sums

    def stat_copy(block):
        return pltpu.make_async_remote_copy(
            src_ref=stat, dst_ref=stat_in.at[b],
            send_sem=stat_send.at[block], recv_sem=stat_recv.at[b],
            device_id=(block, c), device_id_type=MESH,
        )

    def start_stat(k, carry):
        stat_copy((b + k) % nb).start()
        return carry

    repeat(1, nb, start_stat)

    for k in range(1, nc):
        part_copy((c + k) % nc, 0, count).wait_send()

    def add_stat(k, total):
        block = (b + k) % nb
        pltpu.make_async_copy(stat_in.at[block], stat_in.at[block], stat_recv.at[block]).wait()
        return total + stat_in[block]

    sums = lax.fori_loop(1, nb, add_stat, sums)
    curve, mixed, power, norm_now = (sums[:, index : index + 1] for index in range(4))
    alpha = norm_now / curve
    norm_next = norm_now - 2.0 * alpha * mixed + alpha * alpha * power
    changes[0:cols] = alpha * own
    changes[cols : 2 * cols] = alpha * image
    changes[2 * cols : 3 * cols] = (norm_next / norm_now) * own

    def sent_stat(k, carry):
        stat_copy((b + k) % nb).wait_send()
        return carry

    repeat(1, nb, sent_stat)


def local(nb, nc, points, lengths, noise, outscale, solution, residual, direction):
    dim, count = points.shape
    cols = direction.shape[0]
    per = nb // nc
    tile = math.gcd(count, 256)
    tiles = count // tile
    vmem = pl.BlockSpec(memory_space=pltpu.VMEM)
    here = pl.BlockSpec(memory_space=pl.ANY)
    dma = pltpu.SemaphoreType.DMA
    entries = per * count * count
    changes = pl.pallas_call(
        functools.partial(kernel, nb, nc, tile),
        out_shape=jax.ShapeDtypeStruct((3 * cols, count), jnp.float32),
        in_specs=[here] * 6,
        out_specs=vmem,
        scratch_shapes=[
            pltpu.VMEM((dim, count), jnp.float32),
            pltpu.SMEM((dim,), jnp.float32),
            pltpu.VMEM((1, count), jnp.float32),
            pltpu.VMEM((1, 1), jnp.float32),
            pltpu.VMEM((cols, count), jnp.float32),
            pltpu.VMEM((cols, count), jnp.float32),
            dma((6,)),
            pltpu.VMEM((2 * cols, count // 2), jnp.bfloat16),
            pltpu.VMEM((dim, count), jnp.bfloat16),
            pltpu.VMEM((per, nc, 2 * cols, count // 2), jnp.bfloat16),
            pltpu.VMEM((per, dim, count), jnp.bfloat16),
            pltpu.VMEM((count, DEPTH), jnp.bfloat16),
            pltpu.VMEM((DEPTH, count), jnp.bfloat16),
            pltpu.VMEM((2, nc * cols, count), jnp.bfloat16),
            pltpu.VMEM((count, count), jnp.bfloat16),
            pltpu.VMEM((count, count), jnp.bfloat16),
            pltpu.VMEM((nc, cols, count), jnp.float32),
            pltpu.VMEM((nc, cols, count), jnp.float32),
            pltpu.VMEM((cols, 128), jnp.float32),
            pltpu.VMEM((nb, cols, 128), jnp.float32),
            dma((nb,)), dma((per, nc)), dma((nb,)), dma((per,)),
            dma((nc,)), dma((nc,)), dma((nb,)), dma((nb,)),
        ],
        compiler_params=pltpu.CompilerParams(
            collective_id=0, has_side_effects=True, vmem_limit_bytes=56 * 1024 * 1024
        ),
        cost_estimate=pl.CostEstimate(
            flops=2 * entries * (DEPTH + nc * cols), bytes_accessed=1 << 19, transcendentals=2 * entries
        ),
    )(points, lengths, noise.reshape(1, count), outscale.reshape(1, 1), residual, direction)
    after = residual - changes[cols : 2 * cols]
    return (solution + changes[:cols], after, after + changes[2 * cols :])


def solution(mesh):
    in_specs = (
        P(None, "blk"), P(), P("blk"), P(),
        P("col", "blk"), P("col", "blk"), P("col", "blk"),
    )
    out_specs = (P("col", "blk"), P("col", "blk"), P("col", "blk"))
    body = functools.partial(local, mesh.shape["blk"], mesh.shape["col"])
    return jax.shard_map(body, mesh=mesh, in_specs=in_specs, out_specs=out_specs, check_vma=False)
```
